32 devices in a mesh: section: 4 (over y, x), dp: 8 (over z, core).
Axes of the slice: x: 2, y: 2, z: 4, core: 2. Of those that a mesh axis runs over, the one named last changes fastest.
Arguments:
- section_inputs: bfloat16 [4, 1024, 4096], P('section', 'dp'), may hold values from -6 to 6
- gains: float32 [4, 4096], P('section'), may hold values from 0.25 to 1.75
- value_weight: bfloat16 [4, 4096, 1024], P('section', 'dp'), may hold values from -0.09375 to 0.09375
- top_cotangent: bfloat16 [1024, 4096], P('dp'), may hold values from -6 to 6
- proxy_loss: float32 [1024], P('dp'), may hold values from 0.5 to 5.5
- reference_loss: float32 [1024], P('dp'), may hold values from 1 to 3
- lengths: int32 [8, 8], P('dp'), may hold values from 1 to 80, 128 in all within a row
- doc_domain: int32 [8, 8], P('dp'), may hold values from 0 to 21
- log_weights: float32 [22], replicated, may hold values from -4 to -1
- step_count: int32 [1], replicated, may hold values from 1 to 256
Outputs:
- section_grads: bfloat16 [4, 1024, 4096], P('section', 'dp')
- weight_grads: float32 [4, 4096, 1024], P('section', 'dp')
- new_log_weights: float32 [22], replicated
The draws below stay inside these ranges and needn't reach their ends.
Inputs may be any that keep to these rules, and one draw needn't show every extreme that they name: `lengths`: each row sums to 128: the documents fill their pack in order.
All inputs are finite; a program needn't handle non-finite values.
Results may differ from the reference program's by a relative error of at most 0.0071.
Values may be sent and summed in bfloat16 or wider, within the bound.
A program may use at most 128 MiB of HBM per device.

```python
import math
import jax
import jax.numpy as jnp
import numpy as np
from jax import lax

D = 4096
KV = 1024
DOMAINS = 22
DOCS = 8
TOK_DEV = 128
SECTIONS = 4
PACKS = 8
TOKENS = 1024
N_SECTION = 4
N_DP = 8


def draw_proxy_loss(key, part):
    position = jnp.arange(TOKENS, dtype=jnp.float32)
    spread = (1.0 + 2.0 * position / (TOKENS - 1)) / 3.0
    base = jax.random.uniform(key, (TOKENS,), jnp.float32)
    return 0.5 + 5.0 * base * spread


def plant(values, own_key, low, largest):
    longest = values.shape.index(max(values.shape))
    spots = []
    for shift in (0, 1):
        where = [jax.random.randint(jax.random.fold_in(own_key, axis), (), 0, length) for axis, length in enumerate(values.shape)]
        where[longest] = (where[longest] + shift) % values.shape[longest]
        spots.append(tuple(where))
    return values.at[spots[0]].set(low).at[spots[1]].set(largest)


def spiked(result, own_key, source, target, blocks, factor):
    def block_of(dim):
        return (jnp.arange(result.shape[dim]) // (result.shape[dim] // blocks)).reshape((-1,) + (1,) * (result.ndim - 1 - dim))

    near = jax.random.permutation(own_key, blocks)[block_of(target)]
    second = (block_of(target) + blocks // 2) % blocks
    return jnp.where((block_of(source) == near) | (block_of(source) == second), factor * result, result)


def block_scale(own_key, dims, shards, smallest, largest):
    loudness, own = 1.0, jax.random.fold_in(own_key, 6)
    for dim, blocks in shards:
        heights = jnp.exp(jax.random.uniform(jax.random.fold_in(own, dim), (blocks,), jnp.float32, smallest / len(shards), largest / len(shards)))
        loudness = loudness * jnp.repeat(heights, dims[dim] // blocks).reshape([-1 if axis == dim else 1 for axis in range(len(dims))])
    return loudness


def profile(number_of, total, most, slope):
    weights = [(1 << 20) // math.isqrt(standing ** slope) + 1 for standing in range(2, number_of + 1)]
    spare, given = total - most - (number_of - 1), [1] * (number_of - 1)
    while spare > 0:
        candidates = [i for i in range(number_of - 1) if given[i] < most]
        mass, budget = sum([weights[i] for i in candidates]), spare
        for i in candidates:
            addition = min(most - given[i], max(1, budget * weights[i] // mass), spare)
            given[i] = given[i] + addition
            spare = spare - addition
    return np.array([most] + given)


def uneven_parts(own_key, count, total, bound, lean):
    if count == 2:
        one = jax.random.randint(own_key, (), max(1, total - bound), min(bound, total - 1) + 1)
        return jnp.stack([one, total - one])
    sizes = jnp.asarray(profile(count, total, bound, lean), jnp.int32)
    twos = (count - 1) // 2
    giver, sink = sizes[1:1 + 2 * twos:2], sizes[2:2 + 2 * twos:2]
    slack = jnp.minimum(giver - 1, bound - sink)
    moved = jax.random.randint(jax.random.fold_in(own_key, 1), (twos,), 0, 1 << 20) % (slack + 1)
    sizes = sizes.at[1:1 + 2 * twos:2].set(giver - moved).at[2:2 + 2 * twos:2].set(sink + moved)
    return sizes[jax.random.permutation(jax.random.fold_in(own_key, 2), count)]


def bell_draw(rng, shape, scale, limit, split=(), held_as=jnp.bfloat16):
    entries = jax.random.normal(rng, shape, jnp.float32) * scale
    if len(split) > 0:
        entries = block_scale(rng, shape, split, -0.22, 0.18) * entries
    return jnp.clip(entries, min=-limit, max=limit).astype(held_as)


def heavy_noise(rng, shape, deviation, limit, cuts, heavy, kind=jnp.bfloat16):
    entries = deviation * jax.random.normal(rng, shape, jnp.float32)
    if cuts:
        entries = entries * block_scale(rng, shape, cuts, -0.22, 0.18)
    return jnp.clip(spiked(entries, jax.random.fold_in(rng, 3), *heavy), -limit, limit).astype(kind)


def setup_inputs(seed: int = 0) -> dict:
    streams_of = jax.random.split(jax.random.key(seed), 11)
    section_inputs = bell_draw(streams_of[0], (SECTIONS, TOKENS, D), 1.0, 6.0, ((0, 4), (1, 8)))
    gains = jnp.clip(1.0 + 0.15 * jax.random.normal(streams_of[1], (SECTIONS, D), jnp.float32), 0.25, 1.75)
    value_weight = bell_draw(streams_of[2], (SECTIONS, D, KV), D ** -0.5, 0.09375, ((0, 4), (1, 8)))
    top_cotangent = heavy_noise(streams_of[3], (TOKENS, D), 1.0, 6.0, ((0, 8),), (0, 1, 8, 2.0))
    proxy_loss = draw_proxy_loss(jax.random.fold_in(streams_of[10], 71), 0)
    reference_loss = jnp.clip(1.0 + 2.0 * jax.random.uniform(streams_of[5], (TOKENS,), jnp.float32) ** block_scale(streams_of[5], (TOKENS,), ((0, 8),), -0.2, 0.2), 1.0, 3.0)
    lengths = jax.vmap(lambda own: uneven_parts(own, DOCS, TOK_DEV, TOK_DEV // 2 + TOK_DEV // 8, 2))(jax.random.split(streams_of[6], PACKS)).reshape((PACKS, DOCS)).astype(jnp.int32)
    doc_domain = plant(jax.random.randint(streams_of[7], (PACKS, DOCS), 0, DOMAINS), jax.random.fold_in(streams_of[7], 1), 0, DOMAINS - 1).astype(jnp.int32)
    log_weights = jnp.clip(jax.random.uniform(streams_of[8], (DOMAINS,), jnp.float32, -4.0, -1.0), -4.0, -1.0)
    step_count = jax.random.randint(streams_of[9], (1,), 1, 257).astype(jnp.int32)
    return {"section_inputs": section_inputs, "gains": gains, "value_weight": value_weight, "top_cotangent": top_cotangent, "proxy_loss": proxy_loss, "reference_loss": reference_loss, "lengths": lengths, "doc_domain": doc_domain, "log_weights": log_weights, "step_count": step_count}


EPS = 1e-05
SMOOTH = 0.001

def token_weights(proxy_loss, reference_loss, lengths, doc_domain, log_weights, step_count):
    packs = lengths.shape[0]
    per_pack = proxy_loss.shape[0] // packs
    ends = jnp.cumsum(lengths, axis=1).astype(jnp.int32)
    position = jnp.arange(per_pack, dtype=jnp.int32)
    doc_index = lax.optimization_barrier(jnp.sum((position[None, :, None] >= ends[:, None, :]).astype(jnp.int32), axis=2))
    doc_hot = doc_index[:, :, None] == jnp.arange(DOCS, dtype=jnp.int32)[None, None, :]
    end_of = lax.optimization_barrier(jnp.sum(jnp.where(doc_hot, ends[:, None, :], 0), axis=2))
    live = (position[None, :] + 1 != end_of).reshape(-1)
    domain = lax.optimization_barrier(jnp.sum(jnp.where(doc_hot, doc_domain[:, None, :], 0), axis=2)).reshape(-1)
    onehot = (domain[:, None] == jnp.arange(DOMAINS, dtype=jnp.int32)[None, :]).astype(jnp.float32)
    selected = (live & (proxy_loss > reference_loss)).astype(jnp.float32)
    excess = selected * (proxy_loss - reference_loss)
    excess_sum = lax.optimization_barrier(jnp.sum(onehot * excess[:, None], axis=0))
    count = lax.optimization_barrier(jnp.sum(onehot * live.astype(jnp.float32)[:, None], axis=0))
    counts = jnp.maximum(count, 1.0)
    mean_excess = excess_sum / counts
    rate = 1.0 / jnp.sqrt(step_count[0].astype(jnp.float32))
    logits = log_weights + rate * mean_excess
    new_log = logits - jnp.log(jnp.sum(jnp.exp(logits)))
    lam = (1.0 - SMOOTH) * jnp.exp(new_log) + SMOOTH / DOMAINS
    per_domain = lam * proxy_loss.shape[0] / counts
    weight = lax.optimization_barrier(jnp.sum(onehot * per_domain[None, :], axis=1)) * selected
    return (weight, new_log)

def reference(section_inputs, gains, value_weight, top_cotangent, proxy_loss, reference_loss, lengths, doc_domain, log_weights, step_count):
    weight, new_log = token_weights(proxy_loss, reference_loss, lengths, doc_domain, log_weights, step_count)
    cotangent = top_cotangent
    grads_in = []
    grads_w = []
    for section in reversed(range(N_SECTION)):
        xfull = section_inputs[section].astype(jnp.float32)
        gamma = gains[section]
        projection = value_weight[section]
        inverse = lax.rsqrt(lax.optimization_barrier(jnp.mean(xfull * xfull, axis=1, keepdims=True)) + EPS)
        normed = (xfull * inverse * gamma[None, :]).astype(jnp.bfloat16)
        act = jnp.dot(normed, projection, preferred_element_type=jnp.float32)
        hidden = jax.nn.silu(act).astype(jnp.bfloat16)
        grad_h = jnp.dot(cotangent, projection, preferred_element_type=jnp.float32)
        sig = jax.nn.sigmoid(act)
        grad_a = grad_h * sig * (1.0 + act * (1.0 - sig))
        grad_n = jnp.dot(grad_a.astype(jnp.bfloat16), projection.T, preferred_element_type=jnp.float32)
        scaled = gamma[None, :] * grad_n
        grad_x = cotangent.astype(jnp.float32) + inverse * scaled - xfull * inverse ** 3 * lax.optimization_barrier(jnp.mean(xfull * scaled, axis=1, keepdims=True))
        passed = grad_x.astype(jnp.bfloat16)
        grads_in.append((weight[:, None] * passed.astype(jnp.float32)).astype(jnp.bfloat16))
        weighted_a = (weight[:, None] * grad_a).astype(jnp.bfloat16)
        weighted_g = (weight[:, None] * cotangent.astype(jnp.float32)).astype(jnp.bfloat16)
        total = jnp.dot(normed.T, weighted_a, preferred_element_type=jnp.float32) + jnp.dot(weighted_g.T, hidden, preferred_element_type=jnp.float32)
        grads_w.append(total / N_DP)
        cotangent = passed
    section_grads = jnp.stack(grads_in[::-1], axis=0)
    weight_grads = jnp.stack(grads_w[::-1], axis=0)
    return (section_grads, weight_grads, new_log)
```

```python
import functools

import jax
import jax.numpy as jnp
from jax import lax
from jax.experimental import pallas as pl
from jax.experimental.pallas import tpu as pltpu
from jax.sharding import PartitionSpec as P

D = 4096
KV = 1024
DOMAINS = 22
MICRO = 4
LANES = 128
MESH = pl.DeviceIdType.MESH
DOCS = 8


EPS = 1e-05
SMOOTH = 0.001


def passed_along(shard, axis, by):
    size = lax.axis_size(axis)
    pairs = [(i, i + by) for i in range(size) if 0 <= i + by < size]
    return lax.ppermute(shard, axis, pairs)


def local_statistics(proxy_loss, reference_loss, lengths, doc_domain):
    rows = proxy_loss.shape[0]
    ends = jnp.cumsum(lengths[0])
    position = jnp.arange(rows, dtype=jnp.int32)
    doc_index = jnp.sum((position[:, None] >= ends[None, :]).astype(jnp.int32), axis=1)
    doc_hot = doc_index[:, None] == jnp.arange(DOCS, dtype=jnp.int32)[None, :]
    end_of = jnp.sum(jnp.where(doc_hot, ends[None, :], 0), axis=1)
    live = position + 1 != end_of
    domain = jnp.sum(jnp.where(doc_hot, doc_domain[0][None, :], 0), axis=1)
    onehot = (domain[:, None] == jnp.arange(DOMAINS, dtype=jnp.int32)[None, :]).astype(jnp.float32)
    selected = (live & (proxy_loss > reference_loss)).astype(jnp.float32)
    excess = selected * (proxy_loss - reference_loss)
    excess_part = jnp.sum(onehot * excess[:, None], axis=0)
    count_part = jnp.sum(onehot * live.astype(jnp.float32)[:, None], axis=0)
    return (onehot, selected, excess_part, count_part)


def domain_weights(statistics, log_weights, step_count, total_tokens):
    onehot, selected, excess_part, count_part = statistics
    excess_sum, count = lax.psum((excess_part, count_part), "dp")
    counts = jnp.maximum(count, 1.0)
    mean_excess = excess_sum / counts
    rate = 1.0 / jnp.sqrt(step_count[0].astype(jnp.float32))
    logits = log_weights + rate * mean_excess
    new_log = logits - jnp.log(jnp.sum(jnp.exp(logits)))
    lam = (1.0 - SMOOTH) * jnp.exp(new_log) + SMOOTH / DOMAINS
    per_domain = lam * total_tokens / counts
    weight = jnp.sum(onehot * per_domain[None, :], axis=1) * selected
    return (weight, new_log)


def local(
    section_inputs,
    gains,
    value_weight,
    top_cotangent,
    proxy_loss,
    reference_loss,
    lengths,
    doc_domain,
    log_weights,
    step_count,
):
    sections = lax.axis_size("section")
    section = lax.axis_index("section")
    devices = lax.axis_size("dp")
    xfull = section_inputs[0].astype(jnp.float32)
    gamma = gains[0]
    shard = value_weight[0]
    rows = xfull.shape[0]
    block = rows // MICRO
    total_tokens = rows * devices
    statistics = local_statistics(proxy_loss, reference_loss, lengths, doc_domain)
    weight, new_log = domain_weights(statistics, log_weights, step_count, total_tokens)
    inverse = lax.rsqrt(jnp.mean(xfull * xfull, axis=1, keepdims=True) + EPS)
    normed = (xfull * inverse * gamma[None, :]).astype(jnp.bfloat16)
    full_weight = lax.all_gather(shard, "dp", axis=0, tiled=True)
    act = jnp.dot(normed, full_weight, preferred_element_type=jnp.float32)
    hidden = jax.nn.silu(act).astype(jnp.bfloat16)
    kept_cot = jnp.zeros((rows, D), jnp.bfloat16)
    kept_da = jnp.zeros((rows, KV), jnp.float32)
    kept_dx = jnp.zeros((rows, D), jnp.bfloat16)
    state = (kept_cot, kept_da, kept_dx)
    received = jnp.zeros((block, D), jnp.bfloat16)
    ticks = MICRO + sections - 1
    for tick in range(ticks):
        index = tick - (sections - 1) + section
        active = (index >= 0) & (index < MICRO)
        start = jnp.clip(index, 0, MICRO - 1) * block
        top = lax.dynamic_slice_in_dim(top_cotangent, start, block, 0)
        incoming = jnp.where(section == sections - 1, top, received)

        def work(current):
            cot_buf, da_buf, dx_buf = current
            act_part = lax.dynamic_slice_in_dim(act, start, block, 0)
            x_part = lax.dynamic_slice_in_dim(xfull, start, block, 0)
            scale = lax.dynamic_slice_in_dim(inverse, start, block, 0)
            grad_h = jnp.einsum(
                "td,dk->tk", incoming, full_weight, preferred_element_type=jnp.float32
            )
            sig = jax.nn.sigmoid(act_part)
            grad_a = grad_h * sig * (1.0 + act_part * (1.0 - sig))
            grad_n = jnp.einsum(
                "tk,dk->td",
                grad_a.astype(jnp.bfloat16),
                full_weight,
                preferred_element_type=jnp.float32,
            )
            scaled = gamma[None, :] * grad_n
            grad_x = (
                incoming.astype(jnp.float32)
                + scale * scaled
                - x_part * scale**3 * jnp.mean(x_part * scaled, axis=1, keepdims=True)
            )
            passed = grad_x.astype(jnp.bfloat16)
            cot_buf = lax.dynamic_update_slice_in_dim(cot_buf, incoming, start, 0)
            da_buf = lax.dynamic_update_slice_in_dim(da_buf, grad_a, start, 0)
            dx_buf = lax.dynamic_update_slice_in_dim(dx_buf, passed, start, 0)
            return ((cot_buf, da_buf, dx_buf), passed)

        def skip(current):
            return (current, jnp.zeros((block, D), jnp.bfloat16))

        state, outgoing = lax.cond(active, work, skip, state)
        if tick + 1 < ticks:
            received = passed_along(outgoing, "section", -1)
    kept_cot, kept_da, kept_dx = state
    section_grad = (weight[:, None] * kept_dx.astype(jnp.float32)).astype(jnp.bfloat16)
    weighted_a = (weight[:, None] * kept_da).astype(jnp.bfloat16)
    weighted_g = (weight[:, None] * kept_cot.astype(jnp.float32)).astype(jnp.bfloat16)
    total = jnp.einsum("td,tk->dk", normed, weighted_a, preferred_element_type=jnp.float32)
    total = total + jnp.einsum("td,tk->dk", weighted_g, hidden, preferred_element_type=jnp.float32)
    grad_shard = lax.psum_scatter(total / devices, "dp", scatter_dimension=0, tiled=True)
    return (section_grad[None], grad_shard[None], new_log)


def relay_kernel(
    devices,
    sections,
    x_ref,
    gamma_ref,
    shard_ref,
    top_ref,
    stat_ref,
    onehot_ref,
    selected_ref,
    logw_ref,
    rate_ref,
    sg_ref,
    wg_ref,
    log_ref,
    w_full,
    normed,
    cot,
    passed,
    w_cot,
    act,
    dh,
    scaled,
    inverse,
    weight,
    stats,
    hid_full,
    da_full,
    n_col,
    g_col,
    n_colt,
    g_colt,
    w_send,
    w_recv,
    s_send,
    s_recv,
    n_send,
    n_recv,
    h_send,
    h_recv,
    g_send,
    g_recv,
    a_send,
    a_recv,
    f_send,
    f_recv,
    r_send,
    r_recv,
):
    rows, width = x_ref.shape
    depth, kv = shard_ref.shape
    block = rows // MICRO
    chips = devices // 2
    section = lax.axis_index("section")
    me = lax.axis_index("dp")
    chip, core = me // 2, me % 2
    sibling = chip * 2 + (1 - core)

    def tile(i, size):
        return pl.ds(pl.multiple_of(i * size, size), size)

    def remote(src, dst, send, recv, **where):
        return pltpu.make_async_remote_copy(
            src_ref=src, dst_ref=dst, send_sem=send, recv_sem=recv, device_id=where, device_id_type=MESH
        )

    def other(k):
        return lax.rem(me + k, devices)

    def peer(k):
        return lax.rem(chip + k, chips) * 2 + core

    barrier = pltpu.get_barrier_semaphore()
    for k in range(1, devices):
        pl.semaphore_signal(barrier, inc=1, device_id={"dp": other(k)}, device_id_type=MESH)
    for k in (1, sections - 1):
        pl.semaphore_signal(
            barrier, inc=1, device_id={"section": lax.rem(section + k, sections)}, device_id_type=MESH
        )
    pl.semaphore_wait(barrier, devices + 1)

    def w_own(kind, where):
        return remote(shard_ref, w_full.at[tile(me, depth)], w_send.at[kind, me], w_recv.at[me], dp=where)

    def w_copy(kind, j, where):
        view = w_full.at[tile(j, depth)]
        return remote(view, view, w_send.at[kind, j], w_recv.at[j], dp=where)

    up, down = me + 2, me - 2

    @pl.when(chip + 1 < chips)
    def _():
        w_own(0, up).start()

    @pl.when(chip > 0)
    def _():
        w_own(1, down).start()

    w_own(2, sibling).start()

    def s_copy(k):
        return remote(stat_ref, stats.at[me], s_send.at[k], s_recv.at[me], dp=other(k))

    for k in range(1, devices):
        s_copy(k).start()
    stats[me] = stat_ref[...]
    w_full[tile(me, depth), :] = shard_ref[...]

    square = jnp.zeros((rows, 1), jnp.float32)
    for j in range(devices):
        xs = x_ref[:, j * depth : (j + 1) * depth].astype(jnp.float32)
        square = square + jnp.sum(xs * xs, axis=1, keepdims=True)
    inverse[...] = lax.rsqrt(square / width + EPS)

    @pl.loop(0, devices)
    def _(j):
        xs = x_ref[:, tile(j, depth)].astype(jnp.float32)
        normed[:, tile(j, depth)] = (xs * inverse[...] * gamma_ref[:, tile(j, depth)]).astype(jnp.bfloat16)

    is_top = section == sections - 1

    @pl.when(is_top)
    def _():
        cot[...] = top_ref[...]

    act[...] = jnp.zeros_like(act)
    dh[...] = jnp.zeros_like(dh)

    def absorb(j):
        act[...] += jnp.dot(normed[:, tile(j, depth)], w_full[tile(j, depth), :], preferred_element_type=jnp.float32)

        @pl.when(is_top)
        def _():
            dh[...] += jnp.dot(cot[:, tile(j, depth)], w_full[tile(j, depth), :], preferred_element_type=jnp.float32)

    absorb(me)
    w_copy(2, sibling, sibling).wait_recv()
    absorb(sibling)

    for k in range(1, devices):
        j = other(k)
        remote(stats.at[j], stats.at[j], s_send.at[k], s_recv.at[j], dp=sibling).wait_recv()
    total = stats[0]
    for j in range(1, devices):
        total = total + stats[j]
    counts = jnp.maximum(total[1:2], 1.0)
    logits = logw_ref[...] + rate_ref[...] * (total[0:1] / counts)
    valid = lax.broadcasted_iota(jnp.int32, logits.shape, 1) < DOMAINS
    new_log = logits - jnp.log(jnp.sum(jnp.where(valid, jnp.exp(logits), 0.0), axis=1, keepdims=True))
    log_ref[...] = new_log
    lam = (1.0 - SMOOTH) * jnp.exp(new_log) + SMOOTH / DOMAINS
    per_domain = lam * (rows * devices) / counts
    weight[...] = jnp.sum(onehot_ref[...] * per_domain, axis=1, keepdims=True) * selected_ref[...]

    for hop in range(1, chips):
        below, above = me - 2 * hop, me + 2 * hop

        @pl.when(chip >= hop)
        def _():
            w_copy(0, below, sibling).wait_recv()

            @pl.when(chip + 1 < chips)
            def _():
                w_copy(0, below, up).start()

            w_copy(2, below, sibling).start()

        @pl.when(chip + hop < chips)
        def _():
            w_copy(1, above, sibling).wait_recv()

            @pl.when(chip > 0)
            def _():
                w_copy(1, above, down).start()

            w_copy(2, above, sibling).start()

        @pl.when(chip >= hop)
        def _():
            absorb(below)
            j = sibling - 2 * hop
            w_copy(2, j, sibling).wait_recv()
            absorb(j)

        @pl.when(chip + hop < chips)
        def _():
            absorb(above)
            j = sibling + 2 * hop
            w_copy(2, j, sibling).wait_recv()
            absorb(j)

    def n_copy(k):
        j = other(k)
        return remote(
            normed.at[:, tile(j, depth)], n_col.at[tile(me, rows)], n_send.at[k], n_recv.at[me], dp=j
        )

    a = act[...]
    hid_full[tile(me, rows), :] = (a * jax.nn.sigmoid(a)).astype(jnp.bfloat16)
    n_col[tile(me, rows), :] = normed[:, tile(me, depth)]

    def h_copy(k):
        view = hid_full.at[tile(me, rows)]
        return remote(view, view, h_send.at[k], h_recv.at[me], dp=sibling if k == 0 else peer(k))

    for k in range(1, devices):
        n_copy(k).start()
    for k in range(chips):
        h_copy(k).start()

    def r_copy(m):
        return remote(
            passed.at[tile(m, block)], cot.at[tile(m, block)], r_send.at[m], r_recv.at[m], section=section - 1
        )

    def g_copy(k, m):
        j = other(k)
        return remote(
            w_cot.at[tile(m, block), tile(j, depth)],
            g_col.at[tile(me * MICRO + m, block)],
            g_send.at[k, m],
            g_recv.at[me, m],
            dp=j,
        )

    def a_copy(k, m):
        view = da_full.at[tile(me * MICRO + m, block)]
        return remote(view, view, a_send.at[k, m], a_recv.at[me, m], dp=sibling if k == 0 else peer(k))

    @pl.loop(0, MICRO)
    def _(m):
        part = tile(m, block)

        @pl.when(section < sections - 1)
        def _():
            r_copy(m).wait_recv()

            @pl.loop(0, kv // 256)
            def _(n):
                dh[part, tile(n, 256)] = jnp.dot(
                    cot[part, :], w_full[:, tile(n, 256)], preferred_element_type=jnp.float32
                )

        a = act[part, :]
        sig = jax.nn.sigmoid(a)
        grad_a = dh[part, :] * sig * (1.0 + a * (1.0 - sig))
        da_full[tile(me * MICRO + m, block), :] = (weight[part, :] * grad_a).astype(jnp.bfloat16)
        low = grad_a.astype(jnp.bfloat16)

        def back(j, sums):
            grad_n = lax.dot_general(
                low,
                w_full[tile(j, depth), :],
                (((1,), (1,)), ((), ())),
                preferred_element_type=jnp.float32,
            )
            u = gamma_ref[:, tile(j, depth)] * grad_n
            scaled[:, tile(j, depth)] = u
            xs = x_ref[part, tile(j, depth)].astype(jnp.float32)
            return sums + jnp.sum(xs * u, axis=1, keepdims=True)

        sums = lax.fori_loop(0, devices, back, jnp.zeros((block, 1), jnp.float32))
        r = inverse[part, :]
        cube = r * r * r * (sums / width)

        @pl.loop(0, devices)
        def _(j):
            cols = tile(j, depth)
            xs = x_ref[part, cols].astype(jnp.float32)
            g = cot[part, cols].astype(jnp.float32)
            passed[part, cols] = (g + r * scaled[:, cols] - xs * cube).astype(jnp.bfloat16)

        @pl.when(section > 0)
        def _():
            r_copy(m).start()

        for k in range(chips):
            a_copy(k, m).start()

        @pl.loop(0, devices)
        def _(j):
            cols = tile(j, depth)
            w = weight[part, :]
            w_cot[part, cols] = (w * cot[part, cols].astype(jnp.float32)).astype(jnp.bfloat16)
            sg_ref[part, cols] = (w * passed[part, cols].astype(jnp.float32)).astype(jnp.bfloat16)

        for k in range(1, devices):
            g_copy(k, m).start()
        g_col[tile(me * MICRO + m, block), :] = w_cot[part, tile(me, depth)]

    def f_copy(kind, buf, k, src):
        view = buf.at[tile(src, rows)]
        return remote(view, view, f_send.at[kind, k], f_recv.at[kind, k], dp=sibling)

    def h_arrived(j):
        view = hid_full.at[tile(j, rows)]
        remote(view, view, h_send.at[0], h_recv.at[j], dp=sibling).wait_recv()

    def a_arrived(j):
        for m in range(MICRO):
            view = da_full.at[tile(j * MICRO + m, block)]
            remote(view, view, a_send.at[0, m], a_recv.at[j, m], dp=sibling).wait_recv()

    for k in range(1, chips):
        h_arrived(peer(k))
        f_copy(0, hid_full, k, peer(k)).start()
    for k in range(1, devices):
        j = other(k)
        view = n_col.at[tile(j, rows)]
        remote(view, view, n_send.at[k], n_recv.at[j], dp=sibling).wait_recv()

    @pl.loop(0, devices)
    def _(j):
        n_colt[:, tile(j, rows)] = n_col[tile(j, rows), :].T

    for k in range(1, chips):
        a_arrived(peer(k))
        f_copy(1, da_full, k, peer(k)).start()
    h_arrived(sibling)
    a_arrived(sibling)

    for k in range(1, devices):
        j = other(k)
        for m in range(MICRO):
            view = g_col.at[tile(j * MICRO + m, block)]
            remote(view, view, g_send.at[k, m], g_recv.at[j, m], dp=sibling).wait_recv()

    @pl.loop(0, devices)
    def _(j):
        g_colt[:, tile(j, rows)] = g_col[tile(j, rows), :].T

    for k in range(1, chips):
        far = lax.rem(chip + k, chips) * 2 + (1 - core)
        f_copy(0, hid_full, k, far).wait_recv()
        f_copy(1, da_full, k, far).wait_recv()

    @pl.loop(0, kv // 256)
    def _(n):
        cols = tile(n, 256)
        grad = jnp.dot(n_colt[...], da_full[:, cols], preferred_element_type=jnp.float32)
        grad = grad + jnp.dot(g_colt[...], hid_full[:, cols], preferred_element_type=jnp.float32)
        wg_ref[:, cols] = grad / devices

    for k in range(1, devices):
        s_copy(k).wait_send()
        n_copy(k).wait_send()
        for m in range(MICRO):
            g_copy(k, m).wait_send()
    for k in range(chips):
        h_copy(k).wait_send()
        for m in range(MICRO):
            a_copy(k, m).wait_send()
    for k in range(1, chips):
        f_copy(0, hid_full, k, peer(k)).wait_send()
        f_copy(1, da_full, k, peer(k)).wait_send()

    @pl.when(section > 0)
    def _():
        for m in range(MICRO):
            r_copy(m).wait_send()

    @pl.when(chip + 1 < chips)
    def _():
        w_own(0, up).wait_send()

    @pl.when(chip > 0)
    def _():
        w_own(1, down).wait_send()

    w_own(2, sibling).wait_send()
    for hop in range(1, chips):
        below, above = me - 2 * hop, me + 2 * hop

        @pl.when(chip >= hop)
        def _():
            @pl.when(chip + 1 < chips)
            def _():
                w_copy(0, below, up).wait_send()

            w_copy(2, below, sibling).wait_send()

        @pl.when(chip + hop < chips)
        def _():
            @pl.when(chip > 0)
            def _():
                w_copy(1, above, down).wait_send()

            w_copy(2, above, sibling).wait_send()


def fused(
    section_inputs,
    gains,
    value_weight,
    top_cotangent,
    proxy_loss,
    reference_loss,
    lengths,
    doc_domain,
    log_weights,
    step_count,
):
    devices = lax.axis_size("dp")
    sections = lax.axis_size("section")
    rows, width = top_cotangent.shape
    depth, kv = value_weight.shape[1:]
    onehot, selected, excess_part, count_part = local_statistics(
        proxy_loss, reference_loss, lengths, doc_domain
    )
    spare = LANES - DOMAINS
    stat = jnp.pad(jnp.stack([excess_part, count_part]), ((0, 6), (0, spare)))
    rate = 1.0 / jnp.sqrt(step_count.astype(jnp.float32))
    bf, f32 = jnp.bfloat16, jnp.float32
    chips = devices // 2
    dma = pltpu.SemaphoreType.DMA
    flops = 2 * rows * width * kv * 5
    vmem = pl.BlockSpec(memory_space=pltpu.VMEM)
    section_grad, grad_shard, new_log = pl.pallas_call(
        functools.partial(relay_kernel, devices, sections),
        out_shape=(
            jax.ShapeDtypeStruct((rows, width), bf),
            jax.ShapeDtypeStruct((depth, kv), f32),
            jax.ShapeDtypeStruct((1, LANES), f32),
        ),
        in_specs=[vmem] * 9,
        out_specs=(vmem,) * 3,
        scratch_shapes=[
            pltpu.VMEM((width, kv), bf),
            pltpu.VMEM((rows, width), bf),
            pltpu.VMEM((rows, width), bf),
            pltpu.VMEM((rows, width), bf),
            pltpu.VMEM((rows, width), bf),
            pltpu.VMEM((rows, kv), f32),
            pltpu.VMEM((rows, kv), f32),
            pltpu.VMEM((rows // MICRO, width), f32),
            pltpu.VMEM((rows, 1), f32),
            pltpu.VMEM((rows, 1), f32),
            pltpu.VMEM((devices, 8, LANES), f32),
            pltpu.VMEM((rows * devices, kv), bf),
            pltpu.VMEM((rows * devices, kv), bf),
            pltpu.VMEM((rows * devices, depth), bf),
            pltpu.VMEM((rows * devices, depth), bf),
            pltpu.VMEM((depth, rows * devices), bf),
            pltpu.VMEM((depth, rows * devices), bf),
            dma((3, devices)),
            dma((devices,)),
            dma((devices,)),
            dma((devices,)),
            dma((devices,)),
            dma((devices,)),
            dma((chips,)),
            dma((devices,)),
            dma((devices, MICRO)),
            dma((devices, MICRO)),
            dma((chips, MICRO)),
            dma((devices, MICRO)),
            dma((2, chips)),
            dma((2, chips)),
            dma((MICRO,)),
            dma((MICRO,)),
        ],
        compiler_params=pltpu.CompilerParams(
            collective_id=0, has_side_effects=True, vmem_limit_bytes=50 * 2**20
        ),
        cost_estimate=pl.CostEstimate(
            flops=flops, bytes_accessed=2 * width * kv, transcendentals=rows * kv
        ),
    )(
        section_inputs[0],
        gains,
        value_weight[0],
        top_cotangent,
        stat,
        jnp.pad(onehot, ((0, 0), (0, spare))),
        selected[:, None],
        jnp.pad(log_weights, (0, spare))[None],
        jnp.broadcast_to(rate[:, None], (1, LANES)),
    )
    return (section_grad[None], grad_shard[None], new_log[0, :DOMAINS])


def choose(*args):
    depth, kv = args[2].shape[1:]
    devices = lax.axis_size("dp")
    held = 2 * kv * (depth * devices + 2 * args[3].shape[0] * devices)
    if devices % 2 == 0 and depth % LANES == 0 and held <= 2**24:
        return fused(*args)
    return local(*args)


def solution(mesh):
    return jax.shard_map(
        choose,
        mesh=mesh,
        in_specs=(
            P("section", "dp", None),
            P("section", None),
            P("section", "dp", None),
            P("dp", None),
            P("dp"),
            P("dp"),
            P("dp", None),
            P("dp", None),
            P(),
            P(),
        ),
        out_specs=(P("section", "dp", None), P("section", "dp", None), P()),
        check_vma=False,
    )
```

```python
import functools

import jax
import jax.numpy as jnp
from jax import lax
from jax.experimental import pallas as pl
from jax.experimental.pallas import tpu as pltpu
from jax.sharding import PartitionSpec as P

D = 4096
KV = 1024
DOMAINS = 22
MICRO = 4
LANES = 128
MESH = pl.DeviceIdType.MESH
DOCS = 8


EPS = 1e-05
SMOOTH = 0.001


def passed_along(shard, axis, by):
    size = lax.axis_size(axis)
    pairs = [(i, i + by) for i in range(size) if 0 <= i + by < size]
    return lax.ppermute(shard, axis, pairs)


def local_statistics(proxy_loss, reference_loss, lengths, doc_domain):
    rows = proxy_loss.shape[0]
    ends = jnp.cumsum(lengths[0])
    position = jnp.arange(rows, dtype=jnp.int32)
    doc_index = jnp.sum((position[:, None] >= ends[None, :]).astype(jnp.int32), axis=1)
    doc_hot = doc_index[:, None] == jnp.arange(DOCS, dtype=jnp.int32)[None, :]
    end_of = jnp.sum(jnp.where(doc_hot, ends[None, :], 0), axis=1)
    live = position + 1 != end_of
    domain = jnp.sum(jnp.where(doc_hot, doc_domain[0][None, :], 0), axis=1)
    onehot = (domain[:, None] == jnp.arange(DOMAINS, dtype=jnp.int32)[None, :]).astype(jnp.float32)
    selected = (live & (proxy_loss > reference_loss)).astype(jnp.float32)
    excess = selected * (proxy_loss - reference_loss)
    excess_part = jnp.sum(onehot * excess[:, None], axis=0)
    count_part = jnp.sum(onehot * live.astype(jnp.float32)[:, None], axis=0)
    return (onehot, selected, excess_part, count_part)


def domain_weights(statistics, log_weights, step_count, total_tokens):
    onehot, selected, excess_part, count_part = statistics
    excess_sum, count = lax.psum((excess_part, count_part), "dp")
    counts = jnp.maximum(count, 1.0)
    mean_excess = excess_sum / counts
    rate = 1.0 / jnp.sqrt(step_count[0].astype(jnp.float32))
    logits = log_weights + rate * mean_excess
    new_log = logits - jnp.log(jnp.sum(jnp.exp(logits)))
    lam = (1.0 - SMOOTH) * jnp.exp(new_log) + SMOOTH / DOMAINS
    per_domain = lam * total_tokens / counts
    weight = jnp.sum(onehot * per_domain[None, :], axis=1) * selected
    return (weight, new_log)


def local(
    section_inputs,
    gains,
    value_weight,
    top_cotangent,
    proxy_loss,
    reference_loss,
    lengths,
    doc_domain,
    log_weights,
    step_count,
):
    sections = lax.axis_size("section")
    section = lax.axis_index("section")
    devices = lax.axis_size("dp")
    xfull = section_inputs[0].astype(jnp.float32)
    gamma = gains[0]
    shard = value_weight[0]
    rows = xfull.shape[0]
    block = rows // MICRO
    total_tokens = rows * devices
    statistics = local_statistics(proxy_loss, reference_loss, lengths, doc_domain)
    weight, new_log = domain_weights(statistics, log_weights, step_count, total_tokens)
    inverse = lax.rsqrt(jnp.mean(xfull * xfull, axis=1, keepdims=True) + EPS)
    normed = (xfull * inverse * gamma[None, :]).astype(jnp.bfloat16)
    full_weight = lax.all_gather(shard, "dp", axis=0, tiled=True)
    act = jnp.dot(normed, full_weight, preferred_element_type=jnp.float32)
    hidden = jax.nn.silu(act).astype(jnp.bfloat16)
    kept_cot = jnp.zeros((rows, D), jnp.bfloat16)
    kept_da = jnp.zeros((rows, KV), jnp.float32)
    kept_dx = jnp.zeros((rows, D), jnp.bfloat16)
    state = (kept_cot, kept_da, kept_dx)
    received = jnp.zeros((block, D), jnp.bfloat16)
    ticks = MICRO + sections - 1
    for tick in range(ticks):
        index = tick - (sections - 1) + section
        active = (index >= 0) & (index < MICRO)
        start = jnp.clip(index, 0, MICRO - 1) * block
        top = lax.dynamic_slice_in_dim(top_cotangent, start, block, 0)
        incoming = jnp.where(section == sections - 1, top, received)

        def work(current):
            cot_buf, da_buf, dx_buf = current
            act_part = lax.dynamic_slice_in_dim(act, start, block, 0)
            x_part = lax.dynamic_slice_in_dim(xfull, start, block, 0)
            scale = lax.dynamic_slice_in_dim(inverse, start, block, 0)
            grad_h = jnp.einsum(
                "td,dk->tk", incoming, full_weight, preferred_element_type=jnp.float32
            )
            sig = jax.nn.sigmoid(act_part)
            grad_a = grad_h * sig * (1.0 + act_part * (1.0 - sig))
            grad_n = jnp.einsum(
                "tk,dk->td",
                grad_a.astype(jnp.bfloat16),
                full_weight,
                preferred_element_type=jnp.float32,
            )
            scaled = gamma[None, :] * grad_n
            grad_x = (
                incoming.astype(jnp.float32)
                + scale * scaled
                - x_part * scale**3 * jnp.mean(x_part * scaled, axis=1, keepdims=True)
            )
            passed = grad_x.astype(jnp.bfloat16)
            cot_buf = lax.dynamic_update_slice_in_dim(cot_buf, incoming, start, 0)
            da_buf = lax.dynamic_update_slice_in_dim(da_buf, grad_a, start, 0)
            dx_buf = lax.dynamic_update_slice_in_dim(dx_buf, passed, start, 0)
            return ((cot_buf, da_buf, dx_buf), passed)

        def skip(current):
            return (current, jnp.zeros((block, D), jnp.bfloat16))

        state, outgoing = lax.cond(active, work, skip, state)
        if tick + 1 < ticks:
            received = passed_along(outgoing, "section", -1)
    kept_cot, kept_da, kept_dx = state
    section_grad = (weight[:, None] * kept_dx.astype(jnp.float32)).astype(jnp.bfloat16)
    weighted_a = (weight[:, None] * kept_da).astype(jnp.bfloat16)
    weighted_g = (weight[:, None] * kept_cot.astype(jnp.float32)).astype(jnp.bfloat16)
    total = jnp.einsum("td,tk->dk", normed, weighted_a, preferred_element_type=jnp.float32)
    total = total + jnp.einsum("td,tk->dk", weighted_g, hidden, preferred_element_type=jnp.float32)
    grad_shard = lax.psum_scatter(total / devices, "dp", scatter_dimension=0, tiled=True)
    return (section_grad[None], grad_shard[None], new_log)


def relay_kernel(
    devices,
    sections,
    x_hbm,
    gamma_ref,
    shard_ref,
    top_ref,
    proxy_ref,
    refer_ref,
    logw_ref,
    lengths_ref,
    domain_ref,
    step_ref,
    sg_ref,
    wg_ref,
    log_ref,
    x_ref,
    w_full,
    normed,
    cot,
    passed,
    w_cot,
    act,
    dh,
    scaled,
    inverse,
    weight,
    stat_ref,
    stats,
    hid_full,
    da_full,
    n_col,
    g_col,
    n_colt,
    g_colt,
    w_send,
    w_recv,
    s_send,
    s_recv,
    n_send,
    n_recv,
    h_send,
    h_recv,
    g_send,
    g_recv,
    a_send,
    a_recv,
    f_send,
    f_recv,
    r_send,
    r_recv,
    hf_send,
    af_send,
    local_sem,
):
    rows, width = x_hbm.shape
    depth, kv = shard_ref.shape
    block = rows // MICRO
    chips = devices // 2
    section = lax.axis_index("section")
    me = lax.axis_index("dp")
    chip, core = me // 2, me % 2
    sibling = chip * 2 + (1 - core)
    near_by = chips // 2
    side = chip // near_by
    is_near = (chip == near_by) | (chip == near_by - 1)

    def tile(i, size):
        return pl.ds(pl.multiple_of(i * size, size), size)

    def remote(src, dst, send, recv, **where):
        return pltpu.make_async_remote_copy(
            src_ref=src, dst_ref=dst, send_sem=send, recv_sem=recv, device_id=where, device_id_type=MESH
        )

    def other(k):
        return lax.rem(me + k, devices)

    def peer(k):
        return lax.rem(chip + k, chips) * 2 + core

    def same_side(k):
        return (side * near_by + lax.rem(chip - side * near_by + k, near_by)) * 2 + core

    def spread(k):
        if k == 0:
            return sibling
        return same_side(k) if k < near_by else (near_by - side) * 2 + core

    def far_side(q):
        return ((1 - side) * near_by + q) * 2 + core

    is_top = section == sections - 1
    x_in = pltpu.make_async_copy(x_hbm, x_ref, local_sem.at[0])
    w_in = pltpu.make_async_copy(shard_ref, w_full.at[tile(me, depth)], local_sem.at[1])
    top_in = pltpu.make_async_copy(top_ref, cot, local_sem.at[2])
    x_in.start()
    w_in.start()

    @pl.when(is_top)
    def _():
        top_in.start()

    barrier = pltpu.get_barrier_semaphore()
    for k in range(1, devices):
        pl.semaphore_signal(barrier, inc=1, device_id={"dp": other(k)}, device_id_type=MESH)
    for k in (1, sections - 1):
        pl.semaphore_signal(
            barrier, inc=1, device_id={"section": lax.rem(section + k, sections)}, device_id_type=MESH
        )
    pl.semaphore_wait(barrier, devices + 1)

    def w_own(kind, where):
        return remote(shard_ref, w_full.at[tile(me, depth)], w_send.at[kind, me], w_recv.at[me], dp=where)

    def w_copy(kind, j, where):
        view = w_full.at[tile(j, depth)]
        return remote(view, view, w_send.at[kind, j], w_recv.at[j], dp=where)

    up, down = me + 2, me - 2

    @pl.when(chip + 1 < chips)
    def _():
        w_own(0, up).start()

    @pl.when(chip > 0)
    def _():
        w_own(1, down).start()

    w_own(2, sibling).start()

    position = lax.broadcasted_iota(jnp.int32, (rows, 1), 0)
    domain = jnp.zeros((rows, 1), jnp.int32)
    live = jnp.ones((rows, 1), jnp.float32)
    end = 0
    for i in range(DOCS):
        begin = end
        end = begin + lengths_ref[0, i]
        inside = (position >= begin) & (position < end)
        domain = jnp.where(inside, domain_ref[0, i], domain)
        live = jnp.where(inside & (position + 1 == end), 0.0, live)
    gap = proxy_ref[...] - refer_ref[...]
    selected = jnp.where(proxy_ref[...] > refer_ref[...], live, 0.0)
    hot = domain == lax.broadcasted_iota(jnp.int32, (rows, LANES), 1)
    stat_ref[...] = jnp.zeros_like(stat_ref)
    stat_ref[0:1, :] = jnp.sum(jnp.where(hot, selected * gap, 0.0), axis=0, keepdims=True)
    stat_ref[1:2, :] = jnp.sum(jnp.where(hot, live, 0.0), axis=0, keepdims=True)

    def s_copy(k):
        return remote(stat_ref, stats.at[me], s_send.at[k], s_recv.at[me], dp=other(k))

    for k in range(1, devices):
        s_copy(k).start()
    stats[me] = stat_ref[...]
    x_in.wait()

    square = jnp.zeros((rows, 1), jnp.float32)
    for j in range(devices):
        xs = x_ref[:, j * depth : (j + 1) * depth].astype(jnp.float32)
        square = square + jnp.sum(xs * xs, axis=1, keepdims=True)
    inverse[...] = lax.rsqrt(square / width + EPS)

    @pl.loop(0, devices)
    def _(j):
        xs = x_ref[:, tile(j, depth)].astype(jnp.float32)
        normed[:, tile(j, depth)] = (xs * inverse[...] * gamma_ref[:, tile(j, depth)]).astype(jnp.bfloat16)

    @pl.when(is_top)
    def _():
        top_in.wait()

    act[...] = jnp.zeros_like(act)
    dh[...] = jnp.zeros_like(dh)

    def absorb(j):
        act[...] += jnp.dot(normed[:, tile(j, depth)], w_full[tile(j, depth), :], preferred_element_type=jnp.float32)

        @pl.when(is_top)
        def _():
            dh[...] += jnp.dot(cot[:, tile(j, depth)], w_full[tile(j, depth), :], preferred_element_type=jnp.float32)

    w_in.wait()
    absorb(me)
    w_copy(2, sibling, sibling).wait_recv()
    absorb(sibling)

    for k in range(1, devices):
        j = other(k)
        remote(stats.at[j], stats.at[j], s_send.at[k], s_recv.at[j], dp=sibling).wait_recv()
    total = stats[0]
    for j in range(1, devices):
        total = total + stats[j]
    counts = jnp.maximum(total[1:2, :DOMAINS], 1.0)
    rate = 1.0 / jnp.sqrt(jnp.full((1, DOMAINS), step_ref[0], jnp.int32).astype(jnp.float32))
    logits = logw_ref[...] + rate * (total[0:1, :DOMAINS] / counts)
    new_log = logits - jnp.log(jnp.sum(jnp.exp(logits), axis=1, keepdims=True))
    log_ref[...] = new_log
    lam = (1.0 - SMOOTH) * jnp.exp(new_log) + SMOOTH / DOMAINS
    per_domain = lam * (rows * devices) / counts
    hot = domain == lax.broadcasted_iota(jnp.int32, (rows, DOMAINS), 1)
    weight[...] = jnp.sum(jnp.where(hot, per_domain, 0.0), axis=1, keepdims=True) * selected

    for hop in range(1, chips):
        below, above = me - 2 * hop, me + 2 * hop

        @pl.when(chip >= hop)
        def _():
            w_copy(0, below, sibling).wait_recv()

            @pl.when(chip + 1 < chips)
            def _():
                w_copy(0, below, up).start()

            w_copy(2, below, sibling).start()

        @pl.when(chip + hop < chips)
        def _():
            w_copy(1, above, sibling).wait_recv()

            @pl.when(chip > 0)
            def _():
                w_copy(1, above, down).start()

            w_copy(2, above, sibling).start()

        @pl.when(chip >= hop)
        def _():
            absorb(below)
            j = sibling - 2 * hop
            w_copy(2, j, sibling).wait_recv()
            absorb(j)

        @pl.when(chip + hop < chips)
        def _():
            absorb(above)
            j = sibling + 2 * hop
            w_copy(2, j, sibling).wait_recv()
            absorb(j)

    def n_copy(k):
        j = other(k)
        return remote(
            normed.at[:, tile(j, depth)], n_col.at[tile(me, rows)], n_send.at[k], n_recv.at[me], dp=j
        )

    a = act[...]
    hid_full[tile(me, rows), :] = (a * jax.nn.sigmoid(a)).astype(jnp.bfloat16)
    n_col[tile(me, rows), :] = normed[:, tile(me, depth)]

    def h_copy(k):
        view = hid_full.at[tile(me, rows)]
        return remote(view, view, h_send.at[k], h_recv.at[me], dp=spread(k))

    for k in range(near_by + 1):
        h_copy(k).start()
    for k in range(1, devices):
        n_copy(k).start()

    def h_arrived(j):
        view = hid_full.at[tile(j, rows)]
        remote(view, view, h_send.at[0], h_recv.at[j], dp=sibling).wait_recv()

    def a_arrived(j, m):
        view = da_full.at[tile(j * MICRO + m, block)]
        remote(view, view, a_send.at[0, m], a_recv.at[j, m], dp=sibling).wait_recv()

    def hf_copy(q, k):
        j = far_side(q)
        view = hid_full.at[tile(j, rows)]
        return remote(view, view, hf_send.at[q, k], h_recv.at[j], dp=same_side(k))

    def af_copy(q, k, m):
        j = far_side(q)
        view = da_full.at[tile(j * MICRO + m, block)]
        return remote(view, view, af_send.at[q, k, m], a_recv.at[j, m], dp=same_side(k))

    def h_onward():
        @pl.when(is_near)
        def _():
            for q in range(near_by):
                h_arrived(far_side(q))
                for k in range(1, near_by):
                    hf_copy(q, k).start()

    def a_onward(m):
        @pl.when(is_near)
        def _():
            for q in range(near_by):
                a_arrived(far_side(q), m)
                for k in range(1, near_by):
                    af_copy(q, k, m).start()

    def r_copy(m):
        return remote(
            passed.at[tile(m, block)], cot.at[tile(m, block)], r_send.at[m], r_recv.at[m], section=section - 1
        )

    def g_copy(k, m):
        j = other(k)
        return remote(
            w_cot.at[tile(m, block), tile(j, depth)],
            g_col.at[tile(me * MICRO + m, block)],
            g_send.at[k, m],
            g_recv.at[me, m],
            dp=j,
        )

    def a_copy(k, m):
        view = da_full.at[tile(me * MICRO + m, block)]
        return remote(view, view, a_send.at[k, m], a_recv.at[me, m], dp=spread(k))

    @pl.loop(0, MICRO)
    def _(m):
        part = tile(m, block)

        @pl.when(section < sections - 1)
        def _():
            r_copy(m).wait_recv()

            @pl.loop(0, kv // 256)
            def _(n):
                dh[part, tile(n, 256)] = jnp.dot(
                    cot[part, :], w_full[:, tile(n, 256)], preferred_element_type=jnp.float32
                )

        a = act[part, :]
        sig = jax.nn.sigmoid(a)
        grad_a = dh[part, :] * sig * (1.0 + a * (1.0 - sig))
        da_full[tile(me * MICRO + m, block), :] = (weight[part, :] * grad_a).astype(jnp.bfloat16)
        low = grad_a.astype(jnp.bfloat16)

        def back(j, sums):
            grad_n = lax.dot_general(
                low,
                w_full[tile(j, depth), :],
                (((1,), (1,)), ((), ())),
                preferred_element_type=jnp.float32,
            )
            u = gamma_ref[:, tile(j, depth)] * grad_n
            scaled[:, tile(j, depth)] = u
            xs = x_ref[part, tile(j, depth)].astype(jnp.float32)
            return sums + jnp.sum(xs * u, axis=1, keepdims=True)

        sums = lax.fori_loop(0, devices, back, jnp.zeros((block, 1), jnp.float32))
        r = inverse[part, :]
        cube = r * r * r * (sums / width)

        @pl.loop(0, devices)
        def _(j):
            cols = tile(j, depth)
            xs = x_ref[part, cols].astype(jnp.float32)
            g = cot[part, cols].astype(jnp.float32)
            passed[part, cols] = (g + r * scaled[:, cols] - xs * cube).astype(jnp.bfloat16)

        @pl.when(section > 0)
        def _():
            r_copy(m).start()

        for k in range(near_by + 1):
            a_copy(k, m).start()

        @pl.loop(0, devices)
        def _(j):
            cols = tile(j, depth)
            w = weight[part, :]
            w_cot[part, cols] = (w * cot[part, cols].astype(jnp.float32)).astype(jnp.bfloat16)
            sg_ref[part, cols] = (w * passed[part, cols].astype(jnp.float32)).astype(jnp.bfloat16)

        for k in range(1, devices):
            g_copy(k, m).start()
        g_col[tile(me * MICRO + m, block), :] = w_cot[part, tile(me, depth)]

        @pl.when(m == 1)
        def _():
            h_onward()

        @pl.when((section == 0) & (m > 0))
        def _():
            a_onward(m - 1)

    @pl.when(section > 0)
    def _():
        @pl.loop(0, MICRO - 1)
        def _(m):
            a_onward(m)

    a_onward(MICRO - 1)

    def f_copy(kind, buf, k, src):
        view = buf.at[tile(src, rows)]
        return remote(view, view, f_send.at[kind, k], f_recv.at[kind, k], dp=sibling)

    def far(k):
        return lax.rem(chip + k, chips) // near_by != side

    def h_settle(j, seen):
        @pl.when(jnp.logical_not(seen))
        def _():
            h_arrived(j)

    def a_settle(j, seen):
        @pl.when(jnp.logical_not(seen))
        def _():
            for m in range(MICRO):
                a_arrived(j, m)

    for k in range(1, chips):
        h_settle(peer(k), is_near & far(k))
        f_copy(0, hid_full, k, peer(k)).start()
    for k in range(1, devices):
        j = other(k)
        view = n_col.at[tile(j, rows)]
        remote(view, view, n_send.at[k], n_recv.at[j], dp=sibling).wait_recv()

    @pl.loop(0, devices)
    def _(j):
        n_colt[:, tile(j, rows)] = n_col[tile(j, rows), :].T

    for k in range(1, chips):
        a_settle(peer(k), is_near & far(k))
        f_copy(1, da_full, k, peer(k)).start()
    h_arrived(sibling)
    for m in range(MICRO):
        a_arrived(sibling, m)

    for k in range(1, devices):
        j = other(k)
        for m in range(MICRO):
            view = g_col.at[tile(j * MICRO + m, block)]
            remote(view, view, g_send.at[k, m], g_recv.at[j, m], dp=sibling).wait_recv()

    @pl.loop(0, devices)
    def _(j):
        g_colt[:, tile(j, rows)] = g_col[tile(j, rows), :].T

    for k in range(1, chips):
        far = lax.rem(chip + k, chips) * 2 + (1 - core)
        f_copy(0, hid_full, k, far).wait_recv()
        f_copy(1, da_full, k, far).wait_recv()

    @pl.loop(0, kv // 256)
    def _(n):
        cols = tile(n, 256)
        grad = jnp.dot(n_colt[...], da_full[:, cols], preferred_element_type=jnp.float32)
        grad = grad + jnp.dot(g_colt[...], hid_full[:, cols], preferred_element_type=jnp.float32)
        wg_ref[:, cols] = grad / devices

    for k in range(1, devices):
        s_copy(k).wait_send()
        n_copy(k).wait_send()
        for m in range(MICRO):
            g_copy(k, m).wait_send()
    for k in range(near_by + 1):
        h_copy(k).wait_send()
        for m in range(MICRO):
            a_copy(k, m).wait_send()

    @pl.when(is_near)
    def _():
        for q in range(near_by):
            for k in range(1, near_by):
                hf_copy(q, k).wait_send()
                for m in range(MICRO):
                    af_copy(q, k, m).wait_send()

    for k in range(1, chips):
        f_copy(0, hid_full, k, peer(k)).wait_send()
        f_copy(1, da_full, k, peer(k)).wait_send()

    @pl.when(section > 0)
    def _():
        for m in range(MICRO):
            r_copy(m).wait_send()

    @pl.when(chip + 1 < chips)
    def _():
        w_own(0, up).wait_send()

    @pl.when(chip > 0)
    def _():
        w_own(1, down).wait_send()

    w_own(2, sibling).wait_send()
    for hop in range(1, chips):
        below, above = me - 2 * hop, me + 2 * hop

        @pl.when(chip >= hop)
        def _():
            @pl.when(chip + 1 < chips)
            def _():
                w_copy(0, below, up).wait_send()

            w_copy(2, below, sibling).wait_send()

        @pl.when(chip + hop < chips)
        def _():
            @pl.when(chip > 0)
            def _():
                w_copy(1, above, down).wait_send()

            w_copy(2, above, sibling).wait_send()


def fused(
    section_inputs,
    gains,
    value_weight,
    top_cotangent,
    proxy_loss,
    reference_loss,
    lengths,
    doc_domain,
    log_weights,
    step_count,
):
    devices = lax.axis_size("dp")
    sections = lax.axis_size("section")
    rows, width = top_cotangent.shape
    depth, kv = value_weight.shape[1:]
    bf, f32 = jnp.bfloat16, jnp.float32
    chips = devices // 2
    dma = pltpu.SemaphoreType.DMA
    flops = 2 * rows * width * kv * 5
    vmem = pl.BlockSpec(memory_space=pltpu.VMEM)
    smem = pl.BlockSpec(memory_space=pltpu.SMEM)
    any_space = pl.BlockSpec(memory_space=pl.ANY)
    near_by = chips // 2
    section_grad, grad_shard, new_log = pl.pallas_call(
        functools.partial(relay_kernel, devices, sections),
        out_shape=(
            jax.ShapeDtypeStruct((rows, width), bf),
            jax.ShapeDtypeStruct((depth, kv), f32),
            jax.ShapeDtypeStruct((1, DOMAINS), f32),
        ),
        in_specs=[any_space, vmem, any_space, any_space, vmem, vmem, vmem, smem, smem, smem],
        out_specs=(vmem,) * 3,
        scratch_shapes=[
            pltpu.VMEM((rows, width), bf),
            pltpu.VMEM((width, kv), bf),
            pltpu.VMEM((rows, width), bf),
            pltpu.VMEM((rows, width), bf),
            pltpu.VMEM((rows, width), bf),
            pltpu.VMEM((rows, width), bf),
            pltpu.VMEM((rows, kv), f32),
            pltpu.VMEM((rows, kv), f32),
            pltpu.VMEM((rows // MICRO, width), f32),
            pltpu.VMEM((rows, 1), f32),
            pltpu.VMEM((rows, 1), f32),
            pltpu.VMEM((8, LANES), f32),
            pltpu.VMEM((devices, 8, LANES), f32),
            pltpu.VMEM((rows * devices, kv), bf),
            pltpu.VMEM((rows * devices, kv), bf),
            pltpu.VMEM((rows * devices, depth), bf),
            pltpu.VMEM((rows * devices, depth), bf),
            pltpu.VMEM((depth, rows * devices), bf),
            pltpu.VMEM((depth, rows * devices), bf),
            dma((3, devices)),
            dma((devices,)),
            dma((devices,)),
            dma((devices,)),
            dma((devices,)),
            dma((devices,)),
            dma((near_by + 1,)),
            dma((devices,)),
            dma((devices, MICRO)),
            dma((devices, MICRO)),
            dma((near_by + 1, MICRO)),
            dma((devices, MICRO)),
            dma((2, chips)),
            dma((2, chips)),
            dma((MICRO,)),
            dma((MICRO,)),
            dma((near_by, near_by)),
            dma((near_by, near_by, MICRO)),
            dma((3,)),
        ],
        compiler_params=pltpu.CompilerParams(
            collective_id=0, has_side_effects=True, vmem_limit_bytes=50 * 2**20
        ),
        cost_estimate=pl.CostEstimate(
            flops=flops, bytes_accessed=2 * width * kv, transcendentals=rows * kv
        ),
    )(
        section_inputs[0],
        gains,
        value_weight[0],
        top_cotangent,
        proxy_loss[:, None],
        reference_loss[:, None],
        log_weights[None],
        lengths,
        doc_domain,
        step_count,
    )
    return (section_grad[None], grad_shard[None], new_log[0])


def choose(*args):
    depth, kv = args[2].shape[1:]
    devices = lax.axis_size("dp")
    held = 2 * kv * (depth * devices + 2 * args[3].shape[0] * devices)
    if devices % 4 == 0 and depth % LANES == 0 and held <= 2**24:
        return fused(*args)
    return local(*args)


def solution(mesh):
    return jax.shard_map(
        choose,
        mesh=mesh,
        in_specs=(
            P("section", "dp", None),
            P("section", None),
            P("section", "dp", None),
            P("dp", None),
            P("dp"),
            P("dp"),
            P("dp", None),
            P("dp", None),
            P(),
            P(),
        ),
        out_specs=(P("section", "dp", None), P("section", "dp", None), P()),
        check_vma=False,
    )
```

```python
import functools

import jax
import jax.numpy as jnp
from jax import lax
from jax.experimental import pallas as pl
from jax.experimental.pallas import tpu as pltpu
from jax.sharding import PartitionSpec as P

D = 4096
KV = 1024
DOMAINS = 22
MICRO = 4
LANES = 128
MESH = pl.DeviceIdType.MESH
DOCS = 8


EPS = 1e-05
SMOOTH = 0.001


def passed_along(shard, axis, by):
    size = lax.axis_size(axis)
    pairs = [(i, i + by) for i in range(size) if 0 <= i + by < size]
    return lax.ppermute(shard, axis, pairs)


def local_statistics(proxy_loss, reference_loss, lengths, doc_domain):
    rows = proxy_loss.shape[0]
    ends = jnp.cumsum(lengths[0])
    position = jnp.arange(rows, dtype=jnp.int32)
    doc_index = jnp.sum((position[:, None] >= ends[None, :]).astype(jnp.int32), axis=1)
    doc_hot = doc_index[:, None] == jnp.arange(DOCS, dtype=jnp.int32)[None, :]
    end_of = jnp.sum(jnp.where(doc_hot, ends[None, :], 0), axis=1)
    live = position + 1 != end_of
    domain = jnp.sum(jnp.where(doc_hot, doc_domain[0][None, :], 0), axis=1)
    onehot = (domain[:, None] == jnp.arange(DOMAINS, dtype=jnp.int32)[None, :]).astype(jnp.float32)
    selected = (live & (proxy_loss > reference_loss)).astype(jnp.float32)
    excess = selected * (proxy_loss - reference_loss)
    excess_part = jnp.sum(onehot * excess[:, None], axis=0)
    count_part = jnp.sum(onehot * live.astype(jnp.float32)[:, None], axis=0)
    return (onehot, selected, excess_part, count_part)


def domain_weights(statistics, log_weights, step_count, total_tokens):
    onehot, selected, excess_part, count_part = statistics
    excess_sum, count = lax.psum((excess_part, count_part), "dp")
    counts = jnp.maximum(count, 1.0)
    mean_excess = excess_sum / counts
    rate = 1.0 / jnp.sqrt(step_count[0].astype(jnp.float32))
    logits = log_weights + rate * mean_excess
    new_log = logits - jnp.log(jnp.sum(jnp.exp(logits)))
    lam = (1.0 - SMOOTH) * jnp.exp(new_log) + SMOOTH / DOMAINS
    per_domain = lam * total_tokens / counts
    weight = jnp.sum(onehot * per_domain[None, :], axis=1) * selected
    return (weight, new_log)


def local(
    section_inputs,
    gains,
    value_weight,
    top_cotangent,
    proxy_loss,
    reference_loss,
    lengths,
    doc_domain,
    log_weights,
    step_count,
):
    sections = lax.axis_size("section")
    section = lax.axis_index("section")
    devices = lax.axis_size("dp")
    xfull = section_inputs[0].astype(jnp.float32)
    gamma = gains[0]
    shard = value_weight[0]
    rows = xfull.shape[0]
    block = rows // MICRO
    total_tokens = rows * devices
    statistics = local_statistics(proxy_loss, reference_loss, lengths, doc_domain)
    weight, new_log = domain_weights(statistics, log_weights, step_count, total_tokens)
    inverse = lax.rsqrt(jnp.mean(xfull * xfull, axis=1, keepdims=True) + EPS)
    normed = (xfull * inverse * gamma[None, :]).astype(jnp.bfloat16)
    full_weight = lax.all_gather(shard, "dp", axis=0, tiled=True)
    act = jnp.dot(normed, full_weight, preferred_element_type=jnp.float32)
    hidden = jax.nn.silu(act).astype(jnp.bfloat16)
    kept_cot = jnp.zeros((rows, D), jnp.bfloat16)
    kept_da = jnp.zeros((rows, KV), jnp.float32)
    kept_dx = jnp.zeros((rows, D), jnp.bfloat16)
    state = (kept_cot, kept_da, kept_dx)
    received = jnp.zeros((block, D), jnp.bfloat16)
    ticks = MICRO + sections - 1
    for tick in range(ticks):
        index = tick - (sections - 1) + section
        active = (index >= 0) & (index < MICRO)
        start = jnp.clip(index, 0, MICRO - 1) * block
        top = lax.dynamic_slice_in_dim(top_cotangent, start, block, 0)
        incoming = jnp.where(section == sections - 1, top, received)

        def work(current):
            cot_buf, da_buf, dx_buf = current
            act_part = lax.dynamic_slice_in_dim(act, start, block, 0)
            x_part = lax.dynamic_slice_in_dim(xfull, start, block, 0)
            scale = lax.dynamic_slice_in_dim(inverse, start, block, 0)
            grad_h = jnp.einsum(
                "td,dk->tk", incoming, full_weight, preferred_element_type=jnp.float32
            )
            sig = jax.nn.sigmoid(act_part)
            grad_a = grad_h * sig * (1.0 + act_part * (1.0 - sig))
            grad_n = jnp.einsum(
                "tk,dk->td",
                grad_a.astype(jnp.bfloat16),
                full_weight,
                preferred_element_type=jnp.float32,
            )
            scaled = gamma[None, :] * grad_n
            grad_x = (
                incoming.astype(jnp.float32)
                + scale * scaled
                - x_part * scale**3 * jnp.mean(x_part * scaled, axis=1, keepdims=True)
            )
            passed = grad_x.astype(jnp.bfloat16)
            cot_buf = lax.dynamic_update_slice_in_dim(cot_buf, incoming, start, 0)
            da_buf = lax.dynamic_update_slice_in_dim(da_buf, grad_a, start, 0)
            dx_buf = lax.dynamic_update_slice_in_dim(dx_buf, passed, start, 0)
            return ((cot_buf, da_buf, dx_buf), passed)

        def skip(current):
            return (current, jnp.zeros((block, D), jnp.bfloat16))

        state, outgoing = lax.cond(active, work, skip, state)
        if tick + 1 < ticks:
            received = passed_along(outgoing, "section", -1)
    kept_cot, kept_da, kept_dx = state
    section_grad = (weight[:, None] * kept_dx.astype(jnp.float32)).astype(jnp.bfloat16)
    weighted_a = (weight[:, None] * kept_da).astype(jnp.bfloat16)
    weighted_g = (weight[:, None] * kept_cot.astype(jnp.float32)).astype(jnp.bfloat16)
    total = jnp.einsum("td,tk->dk", normed, weighted_a, preferred_element_type=jnp.float32)
    total = total + jnp.einsum("td,tk->dk", weighted_g, hidden, preferred_element_type=jnp.float32)
    grad_shard = lax.psum_scatter(total / devices, "dp", scatter_dimension=0, tiled=True)
    return (section_grad[None], grad_shard[None], new_log)


def relay_kernel(
    devices,
    sections,
    x_hbm,
    gamma_ref,
    shard_ref,
    top_ref,
    proxy_ref,
    refer_ref,
    logw_ref,
    lengths_ref,
    domain_ref,
    step_ref,
    sg_ref,
    wg_ref,
    log_ref,
    x_ref,
    w_full,
    normed,
    cot,
    passed,
    w_cot,
    act,
    dh,
    scaled,
    inverse,
    weight,
    stat_ref,
    stats,
    hid_full,
    da_full,
    n_col,
    g_col,
    n_colt,
    g_colt,
    w_send,
    w_recv,
    s_send,
    s_recv,
    n_send,
    n_recv,
    h_send,
    h_recv,
    g_send,
    g_recv,
    a_send,
    a_recv,
    f_send,
    f_recv,
    r_send,
    r_recv,
    hf_send,
    af_send,
    local_sem,
    v_send,
    v_recv,
    via,
):
    rows, width = x_hbm.shape
    depth, kv = shard_ref.shape
    block = rows // MICRO
    chips = devices // 2
    section = lax.axis_index("section")
    me = lax.axis_index("dp")
    chip, core = me // 2, me % 2
    sibling = chip * 2 + (1 - core)
    near_by = chips // 2
    side = chip // near_by
    is_near = (chip == near_by) | (chip == near_by - 1)

    def tile(i, size):
        return pl.ds(pl.multiple_of(i * size, size), size)

    def remote(src, dst, send, recv, **where):
        return pltpu.make_async_remote_copy(
            src_ref=src, dst_ref=dst, send_sem=send, recv_sem=recv, device_id=where, device_id_type=MESH
        )

    def other(k):
        return lax.rem(me + k, devices)

    def peer(k):
        return lax.rem(chip + k, chips) * 2 + core

    def same_side(k):
        return (side * near_by + lax.rem(chip - side * near_by + k, near_by)) * 2 + core

    def spread(k):
        if k == 0:
            return sibling
        return same_side(k) if k < near_by else (near_by - side) * 2 + core

    def far_side(q):
        return ((1 - side) * near_by + q) * 2 + core

    is_top = section == sections - 1
    x_in = pltpu.make_async_copy(x_hbm, x_ref, local_sem.at[0])
    w_in = pltpu.make_async_copy(shard_ref, w_full.at[tile(me, depth)], local_sem.at[1])
    top_in = pltpu.make_async_copy(top_ref, cot, local_sem.at[2])
    x_in.start()
    w_in.start()

    @pl.when(is_top)
    def _():
        top_in.start()

    barrier = pltpu.get_barrier_semaphore()
    for k in range(1, devices):
        pl.semaphore_signal(barrier, inc=1, device_id={"dp": other(k)}, device_id_type=MESH)
    for k in range(1, sections):
        pl.semaphore_signal(
            barrier, inc=1, device_id={"section": lax.rem(section + k, sections)}, device_id_type=MESH
        )
    pl.semaphore_wait(barrier, devices + sections - 2)

    early = section >= sections // 2
    partner = lax.rem(section + sections // 2, sections)
    across_early, across_late = depth * 5 // 16 // 16 * 16, depth // 4 // 16 * 16

    def span(j, across, kind):
        start = pl.multiple_of(j * depth, 16)
        if kind == 0:
            return pl.ds(start, depth - across)
        return pl.ds(pl.multiple_of(start + depth - across, 16), across)

    def by_turn(act_on):
        @pl.when(early)
        def _():
            act_on(across_early)

        @pl.when(jnp.logical_not(early))
        def _():
            act_on(across_late)

    up, down = me + 2, me - 2

    def w_own(kind, across, where):
        return remote(
            shard_ref.at[pl.ds(0, depth - across)],
            w_full.at[span(me, across, 0)],
            w_send.at[kind, me],
            w_recv.at[0, me],
            dp=where,
        )

    def w_home(kind, j, across, where):
        view = w_full.at[span(j, across, 0)]
        return remote(view, view, w_send.at[kind, j], w_recv.at[0, j], dp=where)

    def w_side(j):
        view = w_full.at[tile(j, depth)]
        return remote(view, view, w_send.at[2, j], w_recv.at[2, j], dp=sibling)

    def w_side_own():
        return remote(shard_ref, w_full.at[tile(me, depth)], w_send.at[2, me], w_recv.at[2, me], dp=sibling)

    def v_out(across):
        return remote(
            shard_ref.at[pl.ds(depth - across, across)],
            via.at[chip, pl.ds(0, across)],
            v_send.at[3, chip],
            v_recv.at[chip],
            section=partner,
        )

    def v_along(kind, z, across, where):
        view = via.at[z, pl.ds(0, across)]
        return remote(view, view, v_send.at[kind, z], v_recv.at[z], dp=where)

    def v_back(z, across):
        j = z * 2 + core
        return remote(
            via.at[z, pl.ds(0, across)],
            w_full.at[span(j, across, 1)],
            v_send.at[2, z],
            w_recv.at[1, j],
            section=partner,
        )

    def home_start(across):
        @pl.when(chip + 1 < chips)
        def _():
            w_own(0, across, up).start()

        @pl.when(chip > 0)
        def _():
            w_own(1, across, down).start()

    def help_start(across):
        v_along(0, chip, across, sibling).wait_recv()

        @pl.when(chip + 1 < chips)
        def _():
            v_along(0, chip, across, up).start()

        @pl.when(chip > 0)
        def _():
            v_along(1, chip, across, down).start()

    def help_hop(hop, across):
        @pl.when(chip >= hop)
        def _():
            z = chip - hop
            v_along(0, z, across, sibling).wait_recv()

            @pl.when(chip + 1 < chips)
            def _():
                v_along(0, z, across, up).start()

            v_back(z, across).start()

        @pl.when(chip + hop < chips)
        def _():
            z = chip + hop
            v_along(1, z, across, sibling).wait_recv()

            @pl.when(chip > 0)
            def _():
                v_along(1, z, across, down).start()

            v_back(z, across).start()

    by_turn(lambda across: v_out(across).start())

    @pl.when(early)
    def _():
        home_start(across_early)

    w_side_own().start()

    position = lax.broadcasted_iota(jnp.int32, (rows, 1), 0)
    domain = jnp.zeros((rows, 1), jnp.int32)
    live = jnp.ones((rows, 1), jnp.float32)
    end = 0
    for i in range(DOCS):
        begin = end
        end = begin + lengths_ref[0, i]
        inside = (position >= begin) & (position < end)
        domain = jnp.where(inside, domain_ref[0, i], domain)
        live = jnp.where(inside & (position + 1 == end), 0.0, live)
    diagonal = position == lax.broadcasted_iota(jnp.int32, (rows, rows), 1)
    proxy = jnp.sum(jnp.where(diagonal, proxy_ref[...], 0.0), axis=1, keepdims=True)
    refer = jnp.sum(jnp.where(diagonal, refer_ref[...], 0.0), axis=1, keepdims=True)
    gap = proxy - refer
    selected = jnp.where(proxy > refer, live, 0.0)
    hot = domain == lax.broadcasted_iota(jnp.int32, (rows, LANES), 1)
    stat_ref[...] = jnp.zeros_like(stat_ref)
    stat_ref[0:1, :] = jnp.sum(jnp.where(hot, selected * gap, 0.0), axis=0, keepdims=True)
    stat_ref[1:2, :] = jnp.sum(jnp.where(hot, live, 0.0), axis=0, keepdims=True)

    def s_copy(k):
        return remote(stat_ref, stats.at[me], s_send.at[k], s_recv.at[me], dp=other(k))

    for k in range(1, devices):
        s_copy(k).start()
    stats[me] = stat_ref[...]
    x_in.wait()

    square = jnp.zeros((rows, 1), jnp.float32)
    for j in range(devices):
        xs = x_ref[:, j * depth : (j + 1) * depth].astype(jnp.float32)
        square = square + jnp.sum(xs * xs, axis=1, keepdims=True)
    inverse[...] = lax.rsqrt(square / width + EPS)

    @pl.loop(0, devices)
    def _(j):
        xs = x_ref[:, tile(j, depth)].astype(jnp.float32)
        normed[:, tile(j, depth)] = (xs * inverse[...] * gamma_ref[:, tile(j, depth)]).astype(jnp.bfloat16)

    @pl.when(is_top)
    def _():
        top_in.wait()

    act[...] = jnp.zeros_like(act)
    dh[...] = jnp.zeros_like(dh)

    def absorb(j):
        act[...] += jnp.dot(normed[:, tile(j, depth)], w_full[tile(j, depth), :], preferred_element_type=jnp.float32)

        @pl.when(is_top)
        def _():
            dh[...] += jnp.dot(cot[:, tile(j, depth)], w_full[tile(j, depth), :], preferred_element_type=jnp.float32)

    w_in.wait()
    absorb(me)
    w_side(sibling).wait_recv()
    absorb(sibling)

    for k in range(1, devices):
        j = other(k)
        remote(stats.at[j], stats.at[j], s_send.at[k], s_recv.at[j], dp=sibling).wait_recv()
    total = stats[0]
    for j in range(1, devices):
        total = total + stats[j]
    counts = jnp.maximum(total[1:2, :DOMAINS], 1.0)
    rate = 1.0 / jnp.sqrt(jnp.full((1, DOMAINS), step_ref[0], jnp.int32).astype(jnp.float32))
    logits = logw_ref[...] + rate * (total[0:1, :DOMAINS] / counts)
    new_log = logits - jnp.log(jnp.sum(jnp.exp(logits), axis=1, keepdims=True))
    log_ref[...] = new_log
    lam = (1.0 - SMOOTH) * jnp.exp(new_log) + SMOOTH / DOMAINS
    per_domain = lam * (rows * devices) / counts
    hot = domain == lax.broadcasted_iota(jnp.int32, (rows, DOMAINS), 1)
    weight[...] = jnp.sum(jnp.where(hot, per_domain, 0.0), axis=1, keepdims=True) * selected

    @pl.when(jnp.logical_not(early))
    def _():
        help_start(across_early)
        for hop in range(1, chips):
            help_hop(hop, across_early)
        home_start(across_late)

    def home_hop(hop, across):
        below, above = me - 2 * hop, me + 2 * hop

        @pl.when(chip >= hop)
        def _():
            w_home(0, below, across, sibling).wait_recv()

            @pl.when(chip + 1 < chips)
            def _():
                w_home(0, below, across, up).start()

        @pl.when(chip + hop < chips)
        def _():
            w_home(1, above, across, sibling).wait_recv()

            @pl.when(chip > 0)
            def _():
                w_home(1, above, across, down).start()

    def v_arrived(j, across):
        view = w_full.at[span(j, across, 1)]
        remote(view, view, w_send.at[2, j], w_recv.at[1, j], dp=sibling).wait_recv()

    def settle(hop):
        below, above = me - 2 * hop, me + 2 * hop

        @pl.when(chip >= hop)
        def _():
            by_turn(lambda across: v_arrived(below, across))
            w_side(below).start()

        @pl.when(chip + hop < chips)
        def _():
            by_turn(lambda across: v_arrived(above, across))
            w_side(above).start()

        @pl.when(chip >= hop)
        def _():
            absorb(below)
            j = sibling - 2 * hop
            w_side(j).wait_recv()
            absorb(j)

        @pl.when(chip + hop < chips)
        def _():
            absorb(above)
            j = sibling + 2 * hop
            w_side(j).wait_recv()
            absorb(j)

    for hop in range(1, chips):
        by_turn(lambda across: home_hop(hop, across))
        settle(hop)

    @pl.when(early)
    def _():
        help_start(across_late)

    @pl.when(early & jnp.logical_not(is_top))
    def _():
        for hop in range(1, chips):
            help_hop(hop, across_late)

    def help_later(hop):
        @pl.when(is_top & (hop < chips))
        def _():
            help_hop(hop, across_late)

    def n_copy(k):
        j = other(k)
        return remote(
            normed.at[:, tile(j, depth)], n_col.at[tile(me, rows)], n_send.at[k], n_recv.at[me], dp=j
        )

    a = act[...]
    hid_full[tile(me, rows), :] = (a * jax.nn.sigmoid(a)).astype(jnp.bfloat16)
    n_col[tile(me, rows), :] = normed[:, tile(me, depth)]

    def h_copy(k):
        view = hid_full.at[tile(me, rows)]
        return remote(view, view, h_send.at[k], h_recv.at[me], dp=spread(k))

    def share():
        for k in range(near_by + 1):
            h_copy(k).start()
        for k in range(1, devices):
            n_copy(k).start()

    @pl.when(jnp.logical_not(is_top))
    def _():
        share()

    def h_arrived(j):
        view = hid_full.at[tile(j, rows)]
        remote(view, view, h_send.at[0], h_recv.at[j], dp=sibling).wait_recv()

    def a_arrived(j, m):
        view = da_full.at[tile(j * MICRO + m, block)]
        remote(view, view, a_send.at[0, m], a_recv.at[j, m], dp=sibling).wait_recv()

    def hf_copy(q, k):
        j = far_side(q)
        view = hid_full.at[tile(j, rows)]
        return remote(view, view, hf_send.at[q, k], h_recv.at[j], dp=same_side(k))

    def af_copy(q, k, m):
        j = far_side(q)
        view = da_full.at[tile(j * MICRO + m, block)]
        return remote(view, view, af_send.at[q, k, m], a_recv.at[j, m], dp=same_side(k))

    def h_onward():
        @pl.when(is_near)
        def _():
            for q in range(near_by):
                h_arrived(far_side(q))
                for k in range(1, near_by):
                    hf_copy(q, k).start()

    def a_onward(m):
        @pl.when(is_near)
        def _():
            for q in range(near_by):
                a_arrived(far_side(q), m)
                for k in range(1, near_by):
                    af_copy(q, k, m).start()

    def r_copy(m):
        return remote(
            passed.at[tile(m, block)], cot.at[tile(m, block)], r_send.at[m], r_recv.at[m], section=section - 1
        )

    def g_copy(k, m):
        j = other(k)
        return remote(
            w_cot.at[tile(m, block), tile(j, depth)],
            g_col.at[tile(me * MICRO + m, block)],
            g_send.at[k, m],
            g_recv.at[me, m],
            dp=j,
        )

    def a_copy(k, m):
        view = da_full.at[tile(me * MICRO + m, block)]
        return remote(view, view, a_send.at[k, m], a_recv.at[me, m], dp=spread(k))

    @pl.loop(0, MICRO)
    def _(m):
        part = tile(m, block)

        @pl.when(section < sections - 1)
        def _():
            r_copy(m).wait_recv()

            @pl.loop(0, kv // 256)
            def _(n):
                dh[part, tile(n, 256)] = jnp.dot(
                    cot[part, :], w_full[:, tile(n, 256)], preferred_element_type=jnp.float32
                )

        help_later(2 * m + 1)
        a = act[part, :]
        sig = jax.nn.sigmoid(a)
        grad_a = dh[part, :] * sig * (1.0 + a * (1.0 - sig))
        da_full[tile(me * MICRO + m, block), :] = (weight[part, :] * grad_a).astype(jnp.bfloat16)
        low = grad_a.astype(jnp.bfloat16)

        def back(j, sums):
            grad_n = lax.dot_general(
                low,
                w_full[tile(j, depth), :],
                (((1,), (1,)), ((), ())),
                preferred_element_type=jnp.float32,
            )
            u = gamma_ref[:, tile(j, depth)] * grad_n
            scaled[:, tile(j, depth)] = u
            xs = x_ref[part, tile(j, depth)].astype(jnp.float32)
            return sums + jnp.sum(xs * u, axis=1, keepdims=True)

        sums = lax.fori_loop(0, devices, back, jnp.zeros((block, 1), jnp.float32))
        r = inverse[part, :]
        cube = r * r * r * (sums / width)

        @pl.loop(0, devices)
        def _(j):
            cols = tile(j, depth)
            xs = x_ref[part, cols].astype(jnp.float32)
            g = cot[part, cols].astype(jnp.float32)
            passed[part, cols] = (g + r * scaled[:, cols] - xs * cube).astype(jnp.bfloat16)

        @pl.when(section > 0)
        def _():
            r_copy(m).start()

        @pl.loop(0, devices)
        def _(j):
            cols = tile(j, depth)
            w = weight[part, :]
            w_cot[part, cols] = (w * cot[part, cols].astype(jnp.float32)).astype(jnp.bfloat16)
            sg_ref[part, cols] = (w * passed[part, cols].astype(jnp.float32)).astype(jnp.bfloat16)

        g_col[tile(me * MICRO + m, block), :] = w_cot[part, tile(me, depth)]
        help_later(2 * m + 2)

        def hand_out(n):
            for k in range(near_by + 1):
                a_copy(k, n).start()
            for k in range(1, devices):
                g_copy(k, n).start()

        @pl.when(is_top & (m == 1))
        def _():
            share()
            hand_out(0)

        @pl.when(jnp.logical_not(is_top) | (m > 0))
        def _():
            hand_out(m)

        @pl.when(m == jnp.where(is_top, MICRO - 1, 1))
        def _():
            h_onward()

        @pl.when((section == 0) & (m > 0))
        def _():
            a_onward(m - 1)

    @pl.when(section > 0)
    def _():
        @pl.loop(0, MICRO - 1)
        def _(m):
            a_onward(m)

    a_onward(MICRO - 1)

    def f_copy(kind, buf, k, src):
        view = buf.at[tile(src, rows)]
        return remote(view, view, f_send.at[kind, k], f_recv.at[kind, k], dp=sibling)

    def far(k):
        return lax.rem(chip + k, chips) // near_by != side

    def h_settle(j, seen):
        @pl.when(jnp.logical_not(seen))
        def _():
            h_arrived(j)

    def a_settle(j, seen):
        @pl.when(jnp.logical_not(seen))
        def _():
            for m in range(MICRO):
                a_arrived(j, m)

    for k in range(1, chips):
        h_settle(peer(k), is_near & far(k))
        f_copy(0, hid_full, k, peer(k)).start()
    for k in range(1, devices):
        j = other(k)
        view = n_col.at[tile(j, rows)]
        remote(view, view, n_send.at[k], n_recv.at[j], dp=sibling).wait_recv()

    @pl.loop(0, devices)
    def _(j):
        n_colt[:, tile(j, rows)] = n_col[tile(j, rows), :].T

    for k in range(1, chips):
        a_settle(peer(k), is_near & far(k))
        f_copy(1, da_full, k, peer(k)).start()
    h_arrived(sibling)
    for m in range(MICRO):
        a_arrived(sibling, m)

    for k in range(1, devices):
        j = other(k)
        for m in range(MICRO):
            view = g_col.at[tile(j * MICRO + m, block)]
            remote(view, view, g_send.at[k, m], g_recv.at[j, m], dp=sibling).wait_recv()

    @pl.loop(0, devices)
    def _(j):
        g_colt[:, tile(j, rows)] = g_col[tile(j, rows), :].T

    for k in range(1, chips):
        far = lax.rem(chip + k, chips) * 2 + (1 - core)
        f_copy(0, hid_full, k, far).wait_recv()
        f_copy(1, da_full, k, far).wait_recv()

    @pl.loop(0, kv // 256)
    def _(n):
        cols = tile(n, 256)
        grad = jnp.dot(n_colt[...], da_full[:, cols], preferred_element_type=jnp.float32)
        grad = grad + jnp.dot(g_colt[...], hid_full[:, cols], preferred_element_type=jnp.float32)
        wg_ref[:, cols] = grad / devices

    for k in range(1, devices):
        s_copy(k).wait_send()
        n_copy(k).wait_send()
        for m in range(MICRO):
            g_copy(k, m).wait_send()
    for k in range(near_by + 1):
        h_copy(k).wait_send()
        for m in range(MICRO):
            a_copy(k, m).wait_send()

    @pl.when(is_near)
    def _():
        for q in range(near_by):
            for k in range(1, near_by):
                hf_copy(q, k).wait_send()
                for m in range(MICRO):
                    af_copy(q, k, m).wait_send()

    for k in range(1, chips):
        f_copy(0, hid_full, k, peer(k)).wait_send()
        f_copy(1, da_full, k, peer(k)).wait_send()

    @pl.when(section > 0)
    def _():
        for m in range(MICRO):
            r_copy(m).wait_send()

    def line_left(across, their):
        v_out(across).wait_send()

        @pl.when(chip + 1 < chips)
        def _():
            w_own(0, across, up).wait_send()
            v_along(0, chip, their, up).wait_send()

        @pl.when(chip > 0)
        def _():
            w_own(1, across, down).wait_send()
            v_along(1, chip, their, down).wait_send()

        for hop in range(1, chips):
            below, above = me - 2 * hop, me + 2 * hop

            @pl.when(chip >= hop)
            def _():
                @pl.when(chip + 1 < chips)
                def _():
                    w_home(0, below, across, up).wait_send()
                    v_along(0, chip - hop, their, up).wait_send()

                w_side(below).wait_send()
                v_back(chip - hop, their).wait_send()

            @pl.when(chip + hop < chips)
            def _():
                @pl.when(chip > 0)
                def _():
                    w_home(1, above, across, down).wait_send()
                    v_along(1, chip + hop, their, down).wait_send()

                w_side(above).wait_send()
                v_back(chip + hop, their).wait_send()

    @pl.when(early)
    def _():
        line_left(across_early, across_late)

    @pl.when(jnp.logical_not(early))
    def _():
        line_left(across_late, across_early)

    w_side_own().wait_send()


def fused(
    section_inputs,
    gains,
    value_weight,
    top_cotangent,
    proxy_loss,
    reference_loss,
    lengths,
    doc_domain,
    log_weights,
    step_count,
):
    devices = lax.axis_size("dp")
    sections = lax.axis_size("section")
    rows, width = top_cotangent.shape
    depth, kv = value_weight.shape[1:]
    bf, f32 = jnp.bfloat16, jnp.float32
    chips = devices // 2
    dma = pltpu.SemaphoreType.DMA
    flops = 2 * rows * width * kv * 5
    vmem = pl.BlockSpec(memory_space=pltpu.VMEM)
    smem = pl.BlockSpec(memory_space=pltpu.SMEM)
    any_space = pl.BlockSpec(memory_space=pl.ANY)
    near_by = chips // 2
    section_grad, grad_shard, new_log = pl.pallas_call(
        functools.partial(relay_kernel, devices, sections),
        out_shape=(
            jax.ShapeDtypeStruct((rows, width), bf),
            jax.ShapeDtypeStruct((depth, kv), f32),
            jax.ShapeDtypeStruct((1, DOMAINS), f32),
        ),
        in_specs=[any_space, vmem, any_space, any_space, vmem, vmem, vmem, smem, smem, smem],
        out_specs=(vmem,) * 3,
        scratch_shapes=[
            pltpu.VMEM((rows, width), bf),
            pltpu.VMEM((width, kv), bf),
            pltpu.VMEM((rows, width), bf),
            pltpu.VMEM((rows, width), bf),
            pltpu.VMEM((rows, width), bf),
            pltpu.VMEM((rows, width), bf),
            pltpu.VMEM((rows, kv), f32),
            pltpu.VMEM((rows, kv), f32),
            pltpu.VMEM((rows // MICRO, width), f32),
            pltpu.VMEM((rows, 1), f32),
            pltpu.VMEM((rows, 1), f32),
            pltpu.VMEM((8, LANES), f32),
            pltpu.VMEM((devices, 8, LANES), f32),
            pltpu.VMEM((rows * devices, kv), bf),
            pltpu.VMEM((rows * devices, kv), bf),
            pltpu.VMEM((rows * devices, depth), bf),
            pltpu.VMEM((rows * devices, depth), bf),
            pltpu.VMEM((depth, rows * devices), bf),
            pltpu.VMEM((depth, rows * devices), bf),
            dma((3, devices)),
            dma((3, devices)),
            dma((devices,)),
            dma((devices,)),
            dma((devices,)),
            dma((devices,)),
            dma((near_by + 1,)),
            dma((devices,)),
            dma((devices, MICRO)),
            dma((devices, MICRO)),
            dma((near_by + 1, MICRO)),
            dma((devices, MICRO)),
            dma((2, chips)),
            dma((2, chips)),
            dma((MICRO,)),
            dma((MICRO,)),
            dma((near_by, near_by)),
            dma((near_by, near_by, MICRO)),
            dma((3,)),
            dma((4, chips)),
            dma((chips,)),
            pltpu.VMEM((chips, depth // 2, kv), bf),
        ],
        compiler_params=pltpu.CompilerParams(
            collective_id=0, has_side_effects=True, vmem_limit_bytes=60 * 2**20
        ),
        cost_estimate=pl.CostEstimate(
            flops=flops, bytes_accessed=2 * width * kv, transcendentals=rows * kv
        ),
    )(
        section_inputs[0],
        gains,
        value_weight[0],
        top_cotangent,
        proxy_loss[None],
        reference_loss[None],
        log_weights[None],
        lengths,
        doc_domain,
        step_count,
    )
    return (section_grad[None], grad_shard[None], new_log[0])


def choose(*args):
    depth, kv = args[2].shape[1:]
    devices = lax.axis_size("dp")
    held = 2 * kv * (depth * devices + 2 * args[3].shape[0] * devices)
    if devices % 4 == 0 and lax.axis_size("section") % 2 == 0 and depth % LANES == 0 and held <= 2**24:
        return fused(*args)
    return local(*args)


def solution(mesh):
    return jax.shard_map(
        choose,
        mesh=mesh,
        in_specs=(
            P("section", "dp", None),
            P("section", None),
            P("section", "dp", None),
            P("dp", None),
            P("dp"),
            P("dp"),
            P("dp", None),
            P("dp", None),
            P(),
            P(),
        ),
        out_specs=(P("section", "dp", None), P("section", "dp", None), P()),
        check_vma=False,
    )
```

```python
import functools

import jax
import jax.numpy as jnp
from jax import lax
from jax.experimental import pallas as pl
from jax.experimental.pallas import tpu as pltpu
from jax.sharding import PartitionSpec as P

D = 4096
KV = 1024
DOMAINS = 22
MICRO = 4
LANES = 128
MESH = pl.DeviceIdType.MESH
DOCS = 8


EPS = 1e-05
SMOOTH = 0.001


def passed_along(shard, axis, by):
    size = lax.axis_size(axis)
    pairs = [(i, i + by) for i in range(size) if 0 <= i + by < size]
    return lax.ppermute(shard, axis, pairs)


def local_statistics(proxy_loss, reference_loss, lengths, doc_domain):
    rows = proxy_loss.shape[0]
    ends = jnp.cumsum(lengths[0])
    position = jnp.arange(rows, dtype=jnp.int32)
    doc_index = jnp.sum((position[:, None] >= ends[None, :]).astype(jnp.int32), axis=1)
    doc_hot = doc_index[:, None] == jnp.arange(DOCS, dtype=jnp.int32)[None, :]
    end_of = jnp.sum(jnp.where(doc_hot, ends[None, :], 0), axis=1)
    live = position + 1 != end_of
    domain = jnp.sum(jnp.where(doc_hot, doc_domain[0][None, :], 0), axis=1)
    onehot = (domain[:, None] == jnp.arange(DOMAINS, dtype=jnp.int32)[None, :]).astype(jnp.float32)
    selected = (live & (proxy_loss > reference_loss)).astype(jnp.float32)
    excess = selected * (proxy_loss - reference_loss)
    excess_part = jnp.sum(onehot * excess[:, None], axis=0)
    count_part = jnp.sum(onehot * live.astype(jnp.float32)[:, None], axis=0)
    return (onehot, selected, excess_part, count_part)


def domain_weights(statistics, log_weights, step_count, total_tokens):
    onehot, selected, excess_part, count_part = statistics
    excess_sum, count = lax.psum((excess_part, count_part), "dp")
    counts = jnp.maximum(count, 1.0)
    mean_excess = excess_sum / counts
    rate = 1.0 / jnp.sqrt(step_count[0].astype(jnp.float32))
    logits = log_weights + rate * mean_excess
    new_log = logits - jnp.log(jnp.sum(jnp.exp(logits)))
    lam = (1.0 - SMOOTH) * jnp.exp(new_log) + SMOOTH / DOMAINS
    per_domain = lam * total_tokens / counts
    weight = jnp.sum(onehot * per_domain[None, :], axis=1) * selected
    return (weight, new_log)


def local(
    section_inputs,
    gains,
    value_weight,
    top_cotangent,
    proxy_loss,
    reference_loss,
    lengths,
    doc_domain,
    log_weights,
    step_count,
):
    sections = lax.axis_size("section")
    section = lax.axis_index("section")
    devices = lax.axis_size("dp")
    xfull = section_inputs[0].astype(jnp.float32)
    gamma = gains[0]
    shard = value_weight[0]
    rows = xfull.shape[0]
    block = rows // MICRO
    total_tokens = rows * devices
    statistics = local_statistics(proxy_loss, reference_loss, lengths, doc_domain)
    weight, new_log = domain_weights(statistics, log_weights, step_count, total_tokens)
    inverse = lax.rsqrt(jnp.mean(xfull * xfull, axis=1, keepdims=True) + EPS)
    normed = (xfull * inverse * gamma[None, :]).astype(jnp.bfloat16)
    full_weight = lax.all_gather(shard, "dp", axis=0, tiled=True)
    act = jnp.dot(normed, full_weight, preferred_element_type=jnp.float32)
    hidden = jax.nn.silu(act).astype(jnp.bfloat16)
    kept_cot = jnp.zeros((rows, D), jnp.bfloat16)
    kept_da = jnp.zeros((rows, KV), jnp.float32)
    kept_dx = jnp.zeros((rows, D), jnp.bfloat16)
    state = (kept_cot, kept_da, kept_dx)
    received = jnp.zeros((block, D), jnp.bfloat16)
    ticks = MICRO + sections - 1
    for tick in range(ticks):
        index = tick - (sections - 1) + section
        active = (index >= 0) & (index < MICRO)
        start = jnp.clip(index, 0, MICRO - 1) * block
        top = lax.dynamic_slice_in_dim(top_cotangent, start, block, 0)
        incoming = jnp.where(section == sections - 1, top, received)

        def work(current):
            cot_buf, da_buf, dx_buf = current
            act_part = lax.dynamic_slice_in_dim(act, start, block, 0)
            x_part = lax.dynamic_slice_in_dim(xfull, start, block, 0)
            scale = lax.dynamic_slice_in_dim(inverse, start, block, 0)
            grad_h = jnp.einsum(
                "td,dk->tk", incoming, full_weight, preferred_element_type=jnp.float32
            )
            sig = jax.nn.sigmoid(act_part)
            grad_a = grad_h * sig * (1.0 + act_part * (1.0 - sig))
            grad_n = jnp.einsum(
                "tk,dk->td",
                grad_a.astype(jnp.bfloat16),
                full_weight,
                preferred_element_type=jnp.float32,
            )
            scaled = gamma[None, :] * grad_n
            grad_x = (
                incoming.astype(jnp.float32)
                + scale * scaled
                - x_part * scale**3 * jnp.mean(x_part * scaled, axis=1, keepdims=True)
            )
            passed = grad_x.astype(jnp.bfloat16)
            cot_buf = lax.dynamic_update_slice_in_dim(cot_buf, incoming, start, 0)
            da_buf = lax.dynamic_update_slice_in_dim(da_buf, grad_a, start, 0)
            dx_buf = lax.dynamic_update_slice_in_dim(dx_buf, passed, start, 0)
            return ((cot_buf, da_buf, dx_buf), passed)

        def skip(current):
            return (current, jnp.zeros((block, D), jnp.bfloat16))

        state, outgoing = lax.cond(active, work, skip, state)
        if tick + 1 < ticks:
            received = passed_along(outgoing, "section", -1)
    kept_cot, kept_da, kept_dx = state
    section_grad = (weight[:, None] * kept_dx.astype(jnp.float32)).astype(jnp.bfloat16)
    weighted_a = (weight[:, None] * kept_da).astype(jnp.bfloat16)
    weighted_g = (weight[:, None] * kept_cot.astype(jnp.float32)).astype(jnp.bfloat16)
    total = jnp.einsum("td,tk->dk", normed, weighted_a, preferred_element_type=jnp.float32)
    total = total + jnp.einsum("td,tk->dk", weighted_g, hidden, preferred_element_type=jnp.float32)
    grad_shard = lax.psum_scatter(total / devices, "dp", scatter_dimension=0, tiled=True)
    return (section_grad[None], grad_shard[None], new_log)


def relay_kernel(
    devices,
    sections,
    x_hbm,
    gamma_ref,
    shard_ref,
    top_ref,
    proxy_ref,
    refer_ref,
    logw_ref,
    lengths_ref,
    domain_ref,
    step_ref,
    sg_ref,
    wg_ref,
    log_ref,
    x_ref,
    w_full,
    normed,
    cot,
    passed,
    w_cot,
    act,
    dh,
    scaled,
    inverse,
    weight,
    stat_ref,
    stats,
    hid_full,
    da_full,
    n_col,
    g_col,
    n_colt,
    g_colt,
    w_send,
    w_recv,
    s_send,
    s_recv,
    n_send,
    n_recv,
    h_send,
    h_recv,
    g_send,
    g_recv,
    a_send,
    a_recv,
    f_send,
    f_recv,
    r_send,
    r_recv,
    hf_send,
    af_send,
    local_sem,
    v_send,
    v_recv,
    via,
):
    rows, width = x_hbm.shape
    depth, kv = shard_ref.shape
    block = rows // MICRO
    chips = devices // 2
    section = lax.axis_index("section")
    me = lax.axis_index("dp")
    chip, core = me // 2, me % 2
    sibling = chip * 2 + (1 - core)
    near_by = chips // 2
    side = chip // near_by
    is_near = (chip == near_by) | (chip == near_by - 1)

    def tile(i, size):
        return pl.ds(pl.multiple_of(i * size, size), size)

    def remote(src, dst, send, recv, **where):
        return pltpu.make_async_remote_copy(
            src_ref=src, dst_ref=dst, send_sem=send, recv_sem=recv, device_id=where, device_id_type=MESH
        )

    def other(k):
        return lax.rem(me + k, devices)

    def peer(k):
        return lax.rem(chip + k, chips) * 2 + core

    def same_side(k):
        return (side * near_by + lax.rem(chip - side * near_by + k, near_by)) * 2 + core

    def spread(k):
        if k == 0:
            return sibling
        return same_side(k) if k < near_by else (near_by - side) * 2 + core

    def far_side(q):
        return ((1 - side) * near_by + q) * 2 + core

    is_top = section == sections - 1
    x_in = pltpu.make_async_copy(x_hbm, x_ref, local_sem.at[0])
    w_in = pltpu.make_async_copy(shard_ref, w_full.at[tile(me, depth)], local_sem.at[1])
    top_in = pltpu.make_async_copy(top_ref, cot, local_sem.at[2])
    x_in.start()
    w_in.start()

    @pl.when(is_top)
    def _():
        top_in.start()

    barrier = pltpu.get_barrier_semaphore()
    for k in range(1, devices):
        pl.semaphore_signal(barrier, inc=1, device_id={"dp": other(k)}, device_id_type=MESH)
    for k in range(1, sections):
        pl.semaphore_signal(
            barrier, inc=1, device_id={"section": lax.rem(section + k, sections)}, device_id_type=MESH
        )
    pl.semaphore_wait(barrier, devices + sections - 2)

    early = section >= sections // 2
    partner = lax.rem(section + sections // 2, sections)
    across_early, across_late = depth * 5 // 16 // 16 * 16, depth * 5 // 16 // 16 * 16

    def span(j, across, kind):
        start = pl.multiple_of(j * depth, 16)
        if kind == 0:
            return pl.ds(start, depth - across)
        return pl.ds(pl.multiple_of(start + depth - across, 16), across)

    def by_turn(act_on):
        @pl.when(early)
        def _():
            act_on(across_early)

        @pl.when(jnp.logical_not(early))
        def _():
            act_on(across_late)

    up, down = me + 2, me - 2

    def w_own(kind, across, where):
        return remote(
            shard_ref.at[pl.ds(0, depth - across)],
            w_full.at[span(me, across, 0)],
            w_send.at[kind, me],
            w_recv.at[0, me],
            dp=where,
        )

    def w_home(kind, j, across, where):
        view = w_full.at[span(j, across, 0)]
        return remote(view, view, w_send.at[kind, j], w_recv.at[0, j], dp=where)

    def w_side(j):
        view = w_full.at[tile(j, depth)]
        return remote(view, view, w_send.at[2, j], w_recv.at[2, j], dp=sibling)

    def w_side_own():
        return remote(shard_ref, w_full.at[tile(me, depth)], w_send.at[2, me], w_recv.at[2, me], dp=sibling)

    def v_out(across):
        return remote(
            shard_ref.at[pl.ds(depth - across, across)],
            via.at[chip, pl.ds(0, across)],
            v_send.at[3, chip],
            v_recv.at[chip],
            section=partner,
        )

    def v_along(kind, z, across, where):
        view = via.at[z, pl.ds(0, across)]
        return remote(view, view, v_send.at[kind, z], v_recv.at[z], dp=where)

    def v_back(z, across):
        j = z * 2 + core
        return remote(
            via.at[z, pl.ds(0, across)],
            w_full.at[span(j, across, 1)],
            v_send.at[2, z],
            w_recv.at[1, j],
            section=partner,
        )

    def home_start(across):
        @pl.when(chip + 1 < chips)
        def _():
            w_own(0, across, up).start()

        @pl.when(chip > 0)
        def _():
            w_own(1, across, down).start()

    def help_start(across):
        v_along(0, chip, across, sibling).wait_recv()

        @pl.when(chip + 1 < chips)
        def _():
            v_along(0, chip, across, up).start()

        @pl.when(chip > 0)
        def _():
            v_along(1, chip, across, down).start()

    def help_hop(hop, across):
        @pl.when(chip >= hop)
        def _():
            z = chip - hop
            v_along(0, z, across, sibling).wait_recv()

            @pl.when(chip + 1 < chips)
            def _():
                v_along(0, z, across, up).start()

            v_back(z, across).start()

        @pl.when(chip + hop < chips)
        def _():
            z = chip + hop
            v_along(1, z, across, sibling).wait_recv()

            @pl.when(chip > 0)
            def _():
                v_along(1, z, across, down).start()

            v_back(z, across).start()

    by_turn(lambda across: v_out(across).start())

    @pl.when(early)
    def _():
        home_start(across_early)

    w_side_own().start()

    position = lax.broadcasted_iota(jnp.int32, (rows, 1), 0)
    domain = jnp.zeros((rows, 1), jnp.int32)
    live = jnp.ones((rows, 1), jnp.float32)
    end = 0
    for i in range(DOCS):
        begin = end
        end = begin + lengths_ref[0, i]
        inside = (position >= begin) & (position < end)
        domain = jnp.where(inside, domain_ref[0, i], domain)
        live = jnp.where(inside & (position + 1 == end), 0.0, live)
    diagonal = position == lax.broadcasted_iota(jnp.int32, (rows, rows), 1)
    proxy = jnp.sum(jnp.where(diagonal, proxy_ref[...], 0.0), axis=1, keepdims=True)
    refer = jnp.sum(jnp.where(diagonal, refer_ref[...], 0.0), axis=1, keepdims=True)
    gap = proxy - refer
    selected = jnp.where(proxy > refer, live, 0.0)
    hot = domain == lax.broadcasted_iota(jnp.int32, (rows, LANES), 1)
    stat_ref[...] = jnp.zeros_like(stat_ref)
    stat_ref[0:1, :] = jnp.sum(jnp.where(hot, selected * gap, 0.0), axis=0, keepdims=True)
    stat_ref[1:2, :] = jnp.sum(jnp.where(hot, live, 0.0), axis=0, keepdims=True)

    def s_copy(k):
        return remote(stat_ref, stats.at[me], s_send.at[k], s_recv.at[me], dp=other(k))

    for k in range(1, devices):
        s_copy(k).start()
    stats[me] = stat_ref[...]
    x_in.wait()

    square = jnp.zeros((rows, 1), jnp.float32)
    for j in range(devices):
        xs = x_ref[:, j * depth : (j + 1) * depth].astype(jnp.float32)
        square = square + jnp.sum(xs * xs, axis=1, keepdims=True)
    inverse[...] = lax.rsqrt(square / width + EPS)

    @pl.loop(0, devices)
    def _(j):
        xs = x_ref[:, tile(j, depth)].astype(jnp.float32)
        normed[:, tile(j, depth)] = (xs * inverse[...] * gamma_ref[:, tile(j, depth)]).astype(jnp.bfloat16)

    def n_copy(k):
        j = other(k)
        return remote(
            normed.at[:, tile(j, depth)], n_col.at[tile(me, rows)], n_send.at[k], n_recv.at[me], dp=j
        )

    def share_normed():
        for k in range(1, devices):
            n_copy(k).start()

    @pl.when(jnp.logical_not(early))
    def _():
        share_normed()

    @pl.when(is_top)
    def _():
        top_in.wait()

    act[...] = jnp.zeros_like(act)
    dh[...] = jnp.zeros_like(dh)

    def absorb(j):
        act[...] += jnp.dot(normed[:, tile(j, depth)], w_full[tile(j, depth), :], preferred_element_type=jnp.float32)

        @pl.when(is_top)
        def _():
            dh[...] += jnp.dot(cot[:, tile(j, depth)], w_full[tile(j, depth), :], preferred_element_type=jnp.float32)

    w_in.wait()
    absorb(me)
    w_side(sibling).wait_recv()
    absorb(sibling)

    for k in range(1, devices):
        j = other(k)
        remote(stats.at[j], stats.at[j], s_send.at[k], s_recv.at[j], dp=sibling).wait_recv()
    total = stats[0]
    for j in range(1, devices):
        total = total + stats[j]
    counts = jnp.maximum(total[1:2, :DOMAINS], 1.0)
    rate = 1.0 / jnp.sqrt(jnp.full((1, DOMAINS), step_ref[0], jnp.int32).astype(jnp.float32))
    logits = logw_ref[...] + rate * (total[0:1, :DOMAINS] / counts)
    new_log = logits - jnp.log(jnp.sum(jnp.exp(logits), axis=1, keepdims=True))
    log_ref[...] = new_log
    lam = (1.0 - SMOOTH) * jnp.exp(new_log) + SMOOTH / DOMAINS
    per_domain = lam * (rows * devices) / counts
    hot = domain == lax.broadcasted_iota(jnp.int32, (rows, DOMAINS), 1)
    weight[...] = jnp.sum(jnp.where(hot, per_domain, 0.0), axis=1, keepdims=True) * selected

    @pl.when(jnp.logical_not(early))
    def _():
        help_start(across_early)
        for hop in range(1, chips - 1):
            help_hop(hop, across_early)
        home_start(across_late)
        help_hop(chips - 1, across_early)

    def home_hop(hop, across):
        below, above = me - 2 * hop, me + 2 * hop

        @pl.when(chip >= hop)
        def _():
            w_home(0, below, across, sibling).wait_recv()

            @pl.when(chip + 1 < chips)
            def _():
                w_home(0, below, across, up).start()

        @pl.when(chip + hop < chips)
        def _():
            w_home(1, above, across, sibling).wait_recv()

            @pl.when(chip > 0)
            def _():
                w_home(1, above, across, down).start()

    def v_arrived(j, across):
        view = w_full.at[span(j, across, 1)]
        remote(view, view, w_send.at[2, j], w_recv.at[1, j], dp=sibling).wait_recv()

    def settle(hop):
        below, above = me - 2 * hop, me + 2 * hop

        @pl.when(chip >= hop)
        def _():
            by_turn(lambda across: v_arrived(below, across))
            w_side(below).start()

        @pl.when(chip + hop < chips)
        def _():
            by_turn(lambda across: v_arrived(above, across))
            w_side(above).start()

        @pl.when(chip >= hop)
        def _():
            absorb(below)
            j = sibling - 2 * hop
            w_side(j).wait_recv()
            absorb(j)

        @pl.when(chip + hop < chips)
        def _():
            absorb(above)
            j = sibling + 2 * hop
            w_side(j).wait_recv()
            absorb(j)

    for hop in range(1, chips):
        by_turn(lambda across: home_hop(hop, across))
        settle(hop)

    @pl.when(early)
    def _():
        help_start(across_late)

    @pl.when(early & jnp.logical_not(is_top))
    def _():
        for hop in range(1, chips):
            help_hop(hop, across_late)

    def help_later(hop):
        @pl.when(is_top & (hop < chips))
        def _():
            help_hop(hop, across_late)

    a = act[...]
    hid_full[tile(me, rows), :] = (a * jax.nn.sigmoid(a)).astype(jnp.bfloat16)
    n_col[tile(me, rows), :] = normed[:, tile(me, depth)]

    def h_copy(k):
        view = hid_full.at[tile(me, rows)]
        return remote(view, view, h_send.at[k], h_recv.at[me], dp=spread(k))

    def share_hidden():
        for k in range(near_by + 1):
            h_copy(k).start()

    @pl.when(jnp.logical_not(is_top))
    def _():
        share_hidden()

    @pl.when(early & jnp.logical_not(is_top))
    def _():
        share_normed()

    def h_arrived(j):
        view = hid_full.at[tile(j, rows)]
        remote(view, view, h_send.at[0], h_recv.at[j], dp=sibling).wait_recv()

    def a_arrived(j, m):
        view = da_full.at[tile(j * MICRO + m, block)]
        remote(view, view, a_send.at[0, m], a_recv.at[j, m], dp=sibling).wait_recv()

    def hf_copy(q, k):
        j = far_side(q)
        view = hid_full.at[tile(j, rows)]
        return remote(view, view, hf_send.at[q, k], h_recv.at[j], dp=same_side(k))

    def af_copy(q, k, m):
        j = far_side(q)
        view = da_full.at[tile(j * MICRO + m, block)]
        return remote(view, view, af_send.at[q, k, m], a_recv.at[j, m], dp=same_side(k))

    def h_onward():
        @pl.when(is_near)
        def _():
            for q in range(near_by):
                h_arrived(far_side(q))
                for k in range(1, near_by):
                    hf_copy(q, k).start()

    def a_onward(m):
        @pl.when(is_near)
        def _():
            for q in range(near_by):
                a_arrived(far_side(q), m)
                for k in range(1, near_by):
                    af_copy(q, k, m).start()

    def r_copy(m):
        return remote(
            passed.at[tile(m, block)], cot.at[tile(m, block)], r_send.at[m], r_recv.at[m], section=section - 1
        )

    def g_copy(k, m):
        j = other(k)
        return remote(
            w_cot.at[tile(m, block), tile(j, depth)],
            g_col.at[tile(me * MICRO + m, block)],
            g_send.at[k, m],
            g_recv.at[me, m],
            dp=j,
        )

    def a_copy(k, m):
        view = da_full.at[tile(me * MICRO + m, block)]
        return remote(view, view, a_send.at[k, m], a_recv.at[me, m], dp=spread(k))

    @pl.loop(0, MICRO)
    def _(m):
        part = tile(m, block)

        @pl.when(section < sections - 1)
        def _():
            r_copy(m).wait_recv()

            @pl.loop(0, kv // 256)
            def _(n):
                dh[part, tile(n, 256)] = jnp.dot(
                    cot[part, :], w_full[:, tile(n, 256)], preferred_element_type=jnp.float32
                )

        help_later(2 * m + 1)
        a = act[part, :]
        sig = jax.nn.sigmoid(a)
        grad_a = dh[part, :] * sig * (1.0 + a * (1.0 - sig))
        da_full[tile(me * MICRO + m, block), :] = (weight[part, :] * grad_a).astype(jnp.bfloat16)
        low = grad_a.astype(jnp.bfloat16)

        def back(j, sums):
            grad_n = lax.dot_general(
                low,
                w_full[tile(j, depth), :],
                (((1,), (1,)), ((), ())),
                preferred_element_type=jnp.float32,
            )
            u = gamma_ref[:, tile(j, depth)] * grad_n
            scaled[:, tile(j, depth)] = u
            xs = x_ref[part, tile(j, depth)].astype(jnp.float32)
            return sums + jnp.sum(xs * u, axis=1, keepdims=True)

        sums = lax.fori_loop(0, devices, back, jnp.zeros((block, 1), jnp.float32))
        r = inverse[part, :]
        cube = r * r * r * (sums / width)

        @pl.loop(0, devices)
        def _(j):
            cols = tile(j, depth)
            xs = x_ref[part, cols].astype(jnp.float32)
            g = cot[part, cols].astype(jnp.float32)
            passed[part, cols] = (g + r * scaled[:, cols] - xs * cube).astype(jnp.bfloat16)

        @pl.when(section > 0)
        def _():
            r_copy(m).start()

        @pl.loop(0, devices)
        def _(j):
            cols = tile(j, depth)
            w = weight[part, :]
            w_cot[part, cols] = (w * cot[part, cols].astype(jnp.float32)).astype(jnp.bfloat16)
            sg_ref[part, cols] = (w * passed[part, cols].astype(jnp.float32)).astype(jnp.bfloat16)

        g_col[tile(me * MICRO + m, block), :] = w_cot[part, tile(me, depth)]
        help_later(2 * m + 2)

        def hand_out(n):
            for k in range(near_by + 1):
                a_copy(k, n).start()
            for k in range(1, devices):
                g_copy(k, n).start()

        @pl.when(is_top & (m == 1))
        def _():
            share_hidden()
            share_normed()
            hand_out(0)

        @pl.when(jnp.logical_not(is_top) | (m > 0))
        def _():
            hand_out(m)

        @pl.when(m == jnp.where(is_top, MICRO - 1, 1))
        def _():
            h_onward()

        @pl.when((section == 0) & (m > 0))
        def _():
            a_onward(m - 1)

    @pl.when(section > 0)
    def _():
        @pl.loop(0, MICRO - 1)
        def _(m):
            a_onward(m)

    a_onward(MICRO - 1)

    def fh_copy(k, src):
        view = hid_full.at[tile(src, rows)]
        return remote(view, view, f_send.at[MICRO, k], f_recv.at[MICRO, k], dp=sibling)

    def fa_copy(k, src, m):
        view = da_full.at[tile(src * MICRO + m, block)]
        return remote(view, view, f_send.at[m, k], f_recv.at[m, k], dp=sibling)

    def far(k):
        return lax.rem(chip + k, chips) // near_by != side

    def h_settle(j, seen):
        @pl.when(jnp.logical_not(seen))
        def _():
            h_arrived(j)

    def a_settle(j, m, seen):
        @pl.when(jnp.logical_not(seen))
        def _():
            a_arrived(j, m)

    for k in range(1, chips):
        h_settle(peer(k), is_near & far(k))
        fh_copy(k, peer(k)).start()
    for k in range(1, devices):
        j = other(k)
        view = n_col.at[tile(j, rows)]
        remote(view, view, n_send.at[k], n_recv.at[j], dp=sibling).wait_recv()

    @pl.loop(0, devices)
    def _(j):
        n_colt[:, tile(j, rows)] = n_col[tile(j, rows), :].T

    @pl.loop(0, MICRO)
    def _(m):
        for k in range(1, chips):
            a_settle(peer(k), m, is_near & far(k))
            fa_copy(k, peer(k), m).start()

    h_arrived(sibling)
    for m in range(MICRO):
        a_arrived(sibling, m)

    for k in range(1, devices):
        j = other(k)
        for m in range(MICRO):
            view = g_col.at[tile(j * MICRO + m, block)]
            remote(view, view, g_send.at[k, m], g_recv.at[j, m], dp=sibling).wait_recv()

    @pl.loop(0, devices)
    def _(j):
        g_colt[:, tile(j, rows)] = g_col[tile(j, rows), :].T

    for k in range(1, chips):
        far = lax.rem(chip + k, chips) * 2 + (1 - core)
        fh_copy(k, far).wait_recv()

    @pl.loop(0, kv // 256)
    def _(n):
        cols = tile(n, 256)
        wg_ref[:, cols] = jnp.dot(g_colt[...], hid_full[:, cols], preferred_element_type=jnp.float32)

    @pl.loop(0, MICRO)
    def _(m):
        for k in range(1, chips):
            far = lax.rem(chip + k, chips) * 2 + (1 - core)
            fa_copy(k, far, m).wait_recv()

    @pl.loop(0, kv // 256)
    def _(n):
        cols = tile(n, 256)
        grad = jnp.dot(n_colt[...], da_full[:, cols], preferred_element_type=jnp.float32)
        wg_ref[:, cols] = (grad + wg_ref[:, cols]) / devices

    for k in range(1, devices):
        s_copy(k).wait_send()
        n_copy(k).wait_send()
        for m in range(MICRO):
            g_copy(k, m).wait_send()
    for k in range(near_by + 1):
        h_copy(k).wait_send()
        for m in range(MICRO):
            a_copy(k, m).wait_send()

    @pl.when(is_near)
    def _():
        for q in range(near_by):
            for k in range(1, near_by):
                hf_copy(q, k).wait_send()
                for m in range(MICRO):
                    af_copy(q, k, m).wait_send()

    for k in range(1, chips):
        fh_copy(k, peer(k)).wait_send()
        for m in range(MICRO):
            fa_copy(k, peer(k), m).wait_send()

    @pl.when(section > 0)
    def _():
        for m in range(MICRO):
            r_copy(m).wait_send()

    def line_left(across, their):
        v_out(across).wait_send()

        @pl.when(chip + 1 < chips)
        def _():
            w_own(0, across, up).wait_send()
            v_along(0, chip, their, up).wait_send()

        @pl.when(chip > 0)
        def _():
            w_own(1, across, down).wait_send()
            v_along(1, chip, their, down).wait_send()

        for hop in range(1, chips):
            below, above = me - 2 * hop, me + 2 * hop

            @pl.when(chip >= hop)
            def _():
                @pl.when(chip + 1 < chips)
                def _():
                    w_home(0, below, across, up).wait_send()
                    v_along(0, chip - hop, their, up).wait_send()

                w_side(below).wait_send()
                v_back(chip - hop, their).wait_send()

            @pl.when(chip + hop < chips)
            def _():
                @pl.when(chip > 0)
                def _():
                    w_home(1, above, across, down).wait_send()
                    v_along(1, chip + hop, their, down).wait_send()

                w_side(above).wait_send()
                v_back(chip + hop, their).wait_send()

    @pl.when(early)
    def _():
        line_left(across_early, across_late)

    @pl.when(jnp.logical_not(early))
    def _():
        line_left(across_late, across_early)

    w_side_own().wait_send()


def fused(
    section_inputs,
    gains,
    value_weight,
    top_cotangent,
    proxy_loss,
    reference_loss,
    lengths,
    doc_domain,
    log_weights,
    step_count,
):
    devices = lax.axis_size("dp")
    sections = lax.axis_size("section")
    rows, width = top_cotangent.shape
    depth, kv = value_weight.shape[1:]
    bf, f32 = jnp.bfloat16, jnp.float32
    chips = devices // 2
    dma = pltpu.SemaphoreType.DMA
    flops = 2 * rows * width * kv * 5
    vmem = pl.BlockSpec(memory_space=pltpu.VMEM)
    smem = pl.BlockSpec(memory_space=pltpu.SMEM)
    any_space = pl.BlockSpec(memory_space=pl.ANY)
    near_by = chips // 2
    section_grad, grad_shard, new_log = pl.pallas_call(
        functools.partial(relay_kernel, devices, sections),
        out_shape=(
            jax.ShapeDtypeStruct((rows, width), bf),
            jax.ShapeDtypeStruct((depth, kv), f32),
            jax.ShapeDtypeStruct((1, DOMAINS), f32),
        ),
        in_specs=[any_space, vmem, any_space, any_space, vmem, vmem, vmem, smem, smem, smem],
        out_specs=(vmem,) * 3,
        scratch_shapes=[
            pltpu.VMEM((rows, width), bf),
            pltpu.VMEM((width, kv), bf),
            pltpu.VMEM((rows, width), bf),
            pltpu.VMEM((rows, width), bf),
            pltpu.VMEM((rows, width), bf),
            pltpu.VMEM((rows, width), bf),
            pltpu.VMEM((rows, kv), f32),
            pltpu.VMEM((rows, kv), f32),
            pltpu.VMEM((rows // MICRO, width), f32),
            pltpu.VMEM((rows, 1), f32),
            pltpu.VMEM((rows, 1), f32),
            pltpu.VMEM((8, LANES), f32),
            pltpu.VMEM((devices, 8, LANES), f32),
            pltpu.VMEM((rows * devices, kv), bf),
            pltpu.VMEM((rows * devices, kv), bf),
            pltpu.VMEM((rows * devices, depth), bf),
            pltpu.VMEM((rows * devices, depth), bf),
            pltpu.VMEM((depth, rows * devices), bf),
            pltpu.VMEM((depth, rows * devices), bf),
            dma((3, devices)),
            dma((3, devices)),
            dma((devices,)),
            dma((devices,)),
            dma((devices,)),
            dma((devices,)),
            dma((near_by + 1,)),
            dma((devices,)),
            dma((devices, MICRO)),
            dma((devices, MICRO)),
            dma((near_by + 1, MICRO)),
            dma((devices, MICRO)),
            dma((MICRO + 1, chips)),
            dma((MICRO + 1, chips)),
            dma((MICRO,)),
            dma((MICRO,)),
            dma((near_by, near_by)),
            dma((near_by, near_by, MICRO)),
            dma((3,)),
            dma((4, chips)),
            dma((chips,)),
            pltpu.VMEM((chips, depth // 2, kv), bf),
        ],
        compiler_params=pltpu.CompilerParams(
            collective_id=0, has_side_effects=True, vmem_limit_bytes=60 * 2**20
        ),
        cost_estimate=pl.CostEstimate(
            flops=flops, bytes_accessed=2 * width * kv, transcendentals=rows * kv
        ),
    )(
        section_inputs[0],
        gains,
        value_weight[0],
        top_cotangent,
        proxy_loss[None],
        reference_loss[None],
        log_weights[None],
        lengths,
        doc_domain,
        step_count,
    )
    return (section_grad[None], grad_shard[None], new_log[0])


def choose(*args):
    depth, kv = args[2].shape[1:]
    devices = lax.axis_size("dp")
    held = 2 * kv * (depth * devices + 2 * args[3].shape[0] * devices)
    if devices % 4 == 0 and lax.axis_size("section") % 2 == 0 and depth % LANES == 0 and held <= 2**24:
        return fused(*args)
    return local(*args)


def solution(mesh):
    return jax.shard_map(
        choose,
        mesh=mesh,
        in_specs=(
            P("section", "dp", None),
            P("section", None),
            P("section", "dp", None),
            P("dp", None),
            P("dp"),
            P("dp"),
            P("dp", None),
            P("dp", None),
            P(),
            P(),
        ),
        out_specs=(P("section", "dp", None), P("section", "dp", None), P()),
        check_vma=False,
    )
```

```python
import functools

import jax
import jax.numpy as jnp
from jax import lax
from jax.experimental import pallas as pl
from jax.experimental.pallas import tpu as pltpu
from jax.sharding import PartitionSpec as P

D = 4096
KV = 1024
DOMAINS = 22
MICRO = 4
LANES = 128
MESH = pl.DeviceIdType.MESH
DOCS = 8


EPS = 1e-05
SMOOTH = 0.001


def passed_along(shard, axis, by):
    size = lax.axis_size(axis)
    pairs = [(i, i + by) for i in range(size) if 0 <= i + by < size]
    return lax.ppermute(shard, axis, pairs)


def local_statistics(proxy_loss, reference_loss, lengths, doc_domain):
    rows = proxy_loss.shape[0]
    ends = jnp.cumsum(lengths[0])
    position = jnp.arange(rows, dtype=jnp.int32)
    doc_index = jnp.sum((position[:, None] >= ends[None, :]).astype(jnp.int32), axis=1)
    doc_hot = doc_index[:, None] == jnp.arange(DOCS, dtype=jnp.int32)[None, :]
    end_of = jnp.sum(jnp.where(doc_hot, ends[None, :], 0), axis=1)
    live = position + 1 != end_of
    domain = jnp.sum(jnp.where(doc_hot, doc_domain[0][None, :], 0), axis=1)
    onehot = (domain[:, None] == jnp.arange(DOMAINS, dtype=jnp.int32)[None, :]).astype(jnp.float32)
    selected = (live & (proxy_loss > reference_loss)).astype(jnp.float32)
    excess = selected * (proxy_loss - reference_loss)
    excess_part = jnp.sum(onehot * excess[:, None], axis=0)
    count_part = jnp.sum(onehot * live.astype(jnp.float32)[:, None], axis=0)
    return (onehot, selected, excess_part, count_part)


def domain_weights(statistics, log_weights, step_count, total_tokens):
    onehot, selected, excess_part, count_part = statistics
    excess_sum, count = lax.psum((excess_part, count_part), "dp")
    counts = jnp.maximum(count, 1.0)
    mean_excess = excess_sum / counts
    rate = 1.0 / jnp.sqrt(step_count[0].astype(jnp.float32))
    logits = log_weights + rate * mean_excess
    new_log = logits - jnp.log(jnp.sum(jnp.exp(logits)))
    lam = (1.0 - SMOOTH) * jnp.exp(new_log) + SMOOTH / DOMAINS
    per_domain = lam * total_tokens / counts
    weight = jnp.sum(onehot * per_domain[None, :], axis=1) * selected
    return (weight, new_log)


def local(
    section_inputs,
    gains,
    value_weight,
    top_cotangent,
    proxy_loss,
    reference_loss,
    lengths,
    doc_domain,
    log_weights,
    step_count,
):
    sections = lax.axis_size("section")
    section = lax.axis_index("section")
    devices = lax.axis_size("dp")
    xfull = section_inputs[0].astype(jnp.float32)
    gamma = gains[0]
    shard = value_weight[0]
    rows = xfull.shape[0]
    block = rows // MICRO
    total_tokens = rows * devices
    statistics = local_statistics(proxy_loss, reference_loss, lengths, doc_domain)
    weight, new_log = domain_weights(statistics, log_weights, step_count, total_tokens)
    inverse = lax.rsqrt(jnp.mean(xfull * xfull, axis=1, keepdims=True) + EPS)
    normed = (xfull * inverse * gamma[None, :]).astype(jnp.bfloat16)
    full_weight = lax.all_gather(shard, "dp", axis=0, tiled=True)
    act = jnp.dot(normed, full_weight, preferred_element_type=jnp.float32)
    hidden = jax.nn.silu(act).astype(jnp.bfloat16)
    kept_cot = jnp.zeros((rows, D), jnp.bfloat16)
    kept_da = jnp.zeros((rows, KV), jnp.float32)
    kept_dx = jnp.zeros((rows, D), jnp.bfloat16)
    state = (kept_cot, kept_da, kept_dx)
    received = jnp.zeros((block, D), jnp.bfloat16)
    ticks = MICRO + sections - 1
    for tick in range(ticks):
        index = tick - (sections - 1) + section
        active = (index >= 0) & (index < MICRO)
        start = jnp.clip(index, 0, MICRO - 1) * block
        top = lax.dynamic_slice_in_dim(top_cotangent, start, block, 0)
        incoming = jnp.where(section == sections - 1, top, received)

        def work(current):
            cot_buf, da_buf, dx_buf = current
            act_part = lax.dynamic_slice_in_dim(act, start, block, 0)
            x_part = lax.dynamic_slice_in_dim(xfull, start, block, 0)
            scale = lax.dynamic_slice_in_dim(inverse, start, block, 0)
            grad_h = jnp.einsum(
                "td,dk->tk", incoming, full_weight, preferred_element_type=jnp.float32
            )
            sig = jax.nn.sigmoid(act_part)
            grad_a = grad_h * sig * (1.0 + act_part * (1.0 - sig))
            grad_n = jnp.einsum(
                "tk,dk->td",
                grad_a.astype(jnp.bfloat16),
                full_weight,
                preferred_element_type=jnp.float32,
            )
            scaled = gamma[None, :] * grad_n
            grad_x = (
                incoming.astype(jnp.float32)
                + scale * scaled
                - x_part * scale**3 * jnp.mean(x_part * scaled, axis=1, keepdims=True)
            )
            passed = grad_x.astype(jnp.bfloat16)
            cot_buf = lax.dynamic_update_slice_in_dim(cot_buf, incoming, start, 0)
            da_buf = lax.dynamic_update_slice_in_dim(da_buf, grad_a, start, 0)
            dx_buf = lax.dynamic_update_slice_in_dim(dx_buf, passed, start, 0)
            return ((cot_buf, da_buf, dx_buf), passed)

        def skip(current):
            return (current, jnp.zeros((block, D), jnp.bfloat16))

        state, outgoing = lax.cond(active, work, skip, state)
        if tick + 1 < ticks:
            received = passed_along(outgoing, "section", -1)
    kept_cot, kept_da, kept_dx = state
    section_grad = (weight[:, None] * kept_dx.astype(jnp.float32)).astype(jnp.bfloat16)
    weighted_a = (weight[:, None] * kept_da).astype(jnp.bfloat16)
    weighted_g = (weight[:, None] * kept_cot.astype(jnp.float32)).astype(jnp.bfloat16)
    total = jnp.einsum("td,tk->dk", normed, weighted_a, preferred_element_type=jnp.float32)
    total = total + jnp.einsum("td,tk->dk", weighted_g, hidden, preferred_element_type=jnp.float32)
    grad_shard = lax.psum_scatter(total / devices, "dp", scatter_dimension=0, tiled=True)
    return (section_grad[None], grad_shard[None], new_log)


def relay_kernel(
    devices,
    sections,
    x_hbm,
    gamma_ref,
    shard_ref,
    top_ref,
    proxy_ref,
    refer_ref,
    logw_ref,
    lengths_ref,
    domain_ref,
    step_ref,
    sg_ref,
    wg_ref,
    log_ref,
    x_ref,
    w_full,
    normed,
    cot,
    passed,
    w_cot,
    act,
    dh,
    scaled,
    inverse,
    weight,
    stat_ref,
    stats,
    hid_full,
    da_full,
    n_col,
    g_col,
    n_colt,
    g_colt,
    w_send,
    w_recv,
    s_send,
    s_recv,
    n_send,
    n_recv,
    h_send,
    h_recv,
    g_send,
    g_recv,
    a_send,
    a_recv,
    f_send,
    f_recv,
    r_send,
    r_recv,
    hf_send,
    af_send,
    local_sem,
    v_send,
    v_recv,
    via,
):
    rows, width = x_hbm.shape
    depth, kv = shard_ref.shape
    block = rows // MICRO
    chips = devices // 2
    section = lax.axis_index("section")
    me = lax.axis_index("dp")
    chip, core = me // 2, me % 2
    sibling = chip * 2 + (1 - core)
    near_by = chips // 2
    side = chip // near_by
    is_near = (chip == near_by) | (chip == near_by - 1)

    def tile(i, size):
        return pl.ds(pl.multiple_of(i * size, size), size)

    def remote(src, dst, send, recv, **where):
        return pltpu.make_async_remote_copy(
            src_ref=src, dst_ref=dst, send_sem=send, recv_sem=recv, device_id=where, device_id_type=MESH
        )

    def other(k):
        return lax.rem(me + k, devices)

    def peer(k):
        return lax.rem(chip + k, chips) * 2 + core

    def same_side(k):
        return (side * near_by + lax.rem(chip - side * near_by + k, near_by)) * 2 + core

    def spread(k):
        if k == 0:
            return sibling
        return same_side(k) if k < near_by else (near_by - side) * 2 + core

    def far_side(q):
        return ((1 - side) * near_by + q) * 2 + core

    is_top = section == sections - 1
    x_in = pltpu.make_async_copy(x_hbm, x_ref, local_sem.at[0])
    w_in = pltpu.make_async_copy(shard_ref, w_full.at[tile(me, depth)], local_sem.at[1])
    top_in = pltpu.make_async_copy(top_ref, cot, local_sem.at[2])
    x_in.start()
    w_in.start()

    @pl.when(is_top)
    def _():
        top_in.start()

    barrier = pltpu.get_barrier_semaphore()
    for k in range(1, devices):
        pl.semaphore_signal(barrier, inc=1, device_id={"dp": other(k)}, device_id_type=MESH)
    for k in range(1, sections):
        pl.semaphore_signal(
            barrier, inc=1, device_id={"section": lax.rem(section + k, sections)}, device_id_type=MESH
        )
    pl.semaphore_wait(barrier, devices + sections - 2)

    early = section >= sections // 2
    partner = lax.rem(section + sections // 2, sections)
    across_early, across_late = depth * 5 // 16 // 16 * 16, depth * 5 // 16 // 16 * 16

    def span(j, across, kind):
        start = pl.multiple_of(j * depth, 16)
        if kind == 0:
            return pl.ds(start, depth - across)
        return pl.ds(pl.multiple_of(start + depth - across, 16), across)

    def by_turn(act_on):
        @pl.when(early)
        def _():
            act_on(across_early)

        @pl.when(jnp.logical_not(early))
        def _():
            act_on(across_late)

    up, down = me + 2, me - 2

    def w_own(kind, across, where):
        return remote(
            shard_ref.at[pl.ds(0, depth - across)],
            w_full.at[span(me, across, 0)],
            w_send.at[kind, me],
            w_recv.at[0, me],
            dp=where,
        )

    def w_home(kind, j, across, where):
        view = w_full.at[span(j, across, 0)]
        return remote(view, view, w_send.at[kind, j], w_recv.at[0, j], dp=where)

    def w_side(j):
        view = w_full.at[tile(j, depth)]
        return remote(view, view, w_send.at[2, j], w_recv.at[2, j], dp=sibling)

    def w_side_own():
        return remote(shard_ref, w_full.at[tile(me, depth)], w_send.at[2, me], w_recv.at[2, me], dp=sibling)

    def v_out(across):
        return remote(
            shard_ref.at[pl.ds(depth - across, across)],
            via.at[chip, pl.ds(0, across)],
            v_send.at[3, chip],
            v_recv.at[chip],
            section=partner,
        )

    def v_along(kind, z, across, where):
        view = via.at[z, pl.ds(0, across)]
        return remote(view, view, v_send.at[kind, z], v_recv.at[z], dp=where)

    def v_back(z, across):
        j = z * 2 + core
        return remote(
            via.at[z, pl.ds(0, across)],
            w_full.at[span(j, across, 1)],
            v_send.at[2, z],
            w_recv.at[1, j],
            section=partner,
        )

    def home_start(across):
        @pl.when(chip + 1 < chips)
        def _():
            w_own(0, across, up).start()

        @pl.when(chip > 0)
        def _():
            w_own(1, across, down).start()

    def help_start(across):
        v_along(0, chip, across, sibling).wait_recv()

        @pl.when(chip + 1 < chips)
        def _():
            v_along(0, chip, across, up).start()

        @pl.when(chip > 0)
        def _():
            v_along(1, chip, across, down).start()

    def help_hop(hop, across):
        @pl.when(chip >= hop)
        def _():
            z = chip - hop
            v_along(0, z, across, sibling).wait_recv()

            @pl.when(chip + 1 < chips)
            def _():
                v_along(0, z, across, up).start()

            v_back(z, across).start()

        @pl.when(chip + hop < chips)
        def _():
            z = chip + hop
            v_along(1, z, across, sibling).wait_recv()

            @pl.when(chip > 0)
            def _():
                v_along(1, z, across, down).start()

            v_back(z, across).start()

    by_turn(lambda across: v_out(across).start())

    at_end = (chip == 0) | (chip == chips - 1)

    @pl.when(early)
    def _():
        home_start(across_early)

    @pl.when(jnp.logical_not(early) & at_end)
    def _():
        home_start(across_late)

    w_side_own().start()

    position = lax.broadcasted_iota(jnp.int32, (rows, 1), 0)
    domain = jnp.zeros((rows, 1), jnp.int32)
    live = jnp.ones((rows, 1), jnp.float32)
    end = 0
    for i in range(DOCS):
        begin = end
        end = begin + lengths_ref[0, i]
        inside = (position >= begin) & (position < end)
        domain = jnp.where(inside, domain_ref[0, i], domain)
        live = jnp.where(inside & (position + 1 == end), 0.0, live)
    diagonal = position == lax.broadcasted_iota(jnp.int32, (rows, rows), 1)
    proxy = jnp.sum(jnp.where(diagonal, proxy_ref[...], 0.0), axis=1, keepdims=True)
    refer = jnp.sum(jnp.where(diagonal, refer_ref[...], 0.0), axis=1, keepdims=True)
    gap = proxy - refer
    selected = jnp.where(proxy > refer, live, 0.0)
    hot = domain == lax.broadcasted_iota(jnp.int32, (rows, LANES), 1)
    stat_ref[...] = jnp.zeros_like(stat_ref)
    stat_ref[0:1, :] = jnp.sum(jnp.where(hot, selected * gap, 0.0), axis=0, keepdims=True)
    stat_ref[1:2, :] = jnp.sum(jnp.where(hot, live, 0.0), axis=0, keepdims=True)

    def s_copy(k):
        return remote(stat_ref, stats.at[me], s_send.at[k], s_recv.at[me], dp=other(k))

    for k in range(1, devices):
        s_copy(k).start()
    stats[me] = stat_ref[...]
    x_in.wait()

    square = jnp.zeros((rows, 1), jnp.float32)
    for j in range(devices):
        xs = x_ref[:, j * depth : (j + 1) * depth].astype(jnp.float32)
        square = square + jnp.sum(xs * xs, axis=1, keepdims=True)
    inverse[...] = lax.rsqrt(square / width + EPS)

    @pl.loop(0, devices)
    def _(j):
        xs = x_ref[:, tile(j, depth)].astype(jnp.float32)
        normed[:, tile(j, depth)] = (xs * inverse[...] * gamma_ref[:, tile(j, depth)]).astype(jnp.bfloat16)

    def n_copy(k):
        j = other(k)
        return remote(
            normed.at[:, tile(j, depth)], n_col.at[tile(me, rows)], n_send.at[k], n_recv.at[me], dp=j
        )

    def share_normed():
        for k in range(1, devices):
            n_copy(k).start()

    @pl.when(is_top)
    def _():
        top_in.wait()

    act[...] = jnp.zeros_like(act)
    dh[...] = jnp.zeros_like(dh)

    def absorb(j):
        act[...] += jnp.dot(normed[:, tile(j, depth)], w_full[tile(j, depth), :], preferred_element_type=jnp.float32)

        @pl.when(is_top)
        def _():
            dh[...] += jnp.dot(cot[:, tile(j, depth)], w_full[tile(j, depth), :], preferred_element_type=jnp.float32)

    w_in.wait()
    absorb(me)
    w_side(sibling).wait_recv()
    absorb(sibling)

    for k in range(1, devices):
        j = other(k)
        remote(stats.at[j], stats.at[j], s_send.at[k], s_recv.at[j], dp=sibling).wait_recv()
    total = stats[0]
    for j in range(1, devices):
        total = total + stats[j]
    counts = jnp.maximum(total[1:2, :DOMAINS], 1.0)
    rate = 1.0 / jnp.sqrt(jnp.full((1, DOMAINS), step_ref[0], jnp.int32).astype(jnp.float32))
    logits = logw_ref[...] + rate * (total[0:1, :DOMAINS] / counts)
    new_log = logits - jnp.log(jnp.sum(jnp.exp(logits), axis=1, keepdims=True))
    log_ref[...] = new_log
    lam = (1.0 - SMOOTH) * jnp.exp(new_log) + SMOOTH / DOMAINS
    per_domain = lam * (rows * devices) / counts
    hot = domain == lax.broadcasted_iota(jnp.int32, (rows, DOMAINS), 1)
    weight[...] = jnp.sum(jnp.where(hot, per_domain, 0.0), axis=1, keepdims=True) * selected

    @pl.when(jnp.logical_not(early))
    def _():
        help_start(across_early)
        for hop in range(1, chips - 1):
            help_hop(hop, across_early)

        @pl.when(jnp.logical_not(at_end))
        def _():
            home_start(across_late)

        help_hop(chips - 1, across_early)

    def home_hop(hop, across):
        below, above = me - 2 * hop, me + 2 * hop

        @pl.when(chip >= hop)
        def _():
            w_home(0, below, across, sibling).wait_recv()

            @pl.when(chip + 1 < chips)
            def _():
                w_home(0, below, across, up).start()

        @pl.when(chip + hop < chips)
        def _():
            w_home(1, above, across, sibling).wait_recv()

            @pl.when(chip > 0)
            def _():
                w_home(1, above, across, down).start()

    def v_arrived(j, across):
        view = w_full.at[span(j, across, 1)]
        remote(view, view, w_send.at[2, j], w_recv.at[1, j], dp=sibling).wait_recv()

    def settle(hop):
        below, above = me - 2 * hop, me + 2 * hop

        @pl.when(chip >= hop)
        def _():
            by_turn(lambda across: v_arrived(below, across))
            w_side(below).start()

        @pl.when(chip + hop < chips)
        def _():
            by_turn(lambda across: v_arrived(above, across))
            w_side(above).start()

        @pl.when(chip >= hop)
        def _():
            absorb(below)
            j = sibling - 2 * hop
            w_side(j).wait_recv()
            absorb(j)

        @pl.when(chip + hop < chips)
        def _():
            absorb(above)
            j = sibling + 2 * hop
            w_side(j).wait_recv()
            absorb(j)

    for hop in range(1, chips):
        by_turn(lambda across: home_hop(hop, across))
        settle(hop)

    @pl.when(early)
    def _():
        help_start(across_late)

    @pl.when(early & jnp.logical_not(is_top))
    def _():
        for hop in range(1, chips):
            help_hop(hop, across_late)

    def help_later(hop):
        @pl.when(is_top & (hop > 0) & (hop < chips))
        def _():
            help_hop(hop, across_late)

    a = act[...]
    hid_full[tile(me, rows), :] = (a * jax.nn.sigmoid(a)).astype(jnp.bfloat16)
    n_col[tile(me, rows), :] = normed[:, tile(me, depth)]

    def h_copy(k):
        view = hid_full.at[tile(me, rows)]
        return remote(view, view, h_send.at[k], h_recv.at[me], dp=spread(k))

    def share_hidden():
        for k in range(near_by + 1):
            h_copy(k).start()

    @pl.when(jnp.logical_not(is_top))
    def _():
        share_hidden()

    @pl.when(jnp.logical_not(is_top))
    def _():
        share_normed()

    def h_arrived(j):
        view = hid_full.at[tile(j, rows)]
        remote(view, view, h_send.at[0], h_recv.at[j], dp=sibling).wait_recv()

    def a_arrived(j, m):
        view = da_full.at[tile(j * MICRO + m, block)]
        remote(view, view, a_send.at[0, m], a_recv.at[j, m], dp=sibling).wait_recv()

    def hf_copy(q, k):
        j = far_side(q)
        view = hid_full.at[tile(j, rows)]
        return remote(view, view, hf_send.at[q, k], h_recv.at[j], dp=same_side(k))

    def af_copy(q, k, m):
        j = far_side(q)
        view = da_full.at[tile(j * MICRO + m, block)]
        return remote(view, view, af_send.at[q, k, m], a_recv.at[j, m], dp=same_side(k))

    def h_onward():
        @pl.when(is_near)
        def _():
            for q in range(near_by):
                h_arrived(far_side(q))
                for k in range(1, near_by):
                    hf_copy(q, k).start()

    def a_onward(m):
        @pl.when(is_near)
        def _():
            for q in range(near_by):
                a_arrived(far_side(q), m)
                for k in range(1, near_by):
                    af_copy(q, k, m).start()

    def r_copy(m):
        return remote(
            passed.at[tile(m, block)], cot.at[tile(m, block)], r_send.at[m], r_recv.at[m], section=section - 1
        )

    def g_copy(k, m):
        j = other(k)
        return remote(
            w_cot.at[tile(m, block), tile(j, depth)],
            g_col.at[tile(me * MICRO + m, block)],
            g_send.at[k, m],
            g_recv.at[me, m],
            dp=j,
        )

    def a_copy(k, m):
        view = da_full.at[tile(me * MICRO + m, block)]
        return remote(view, view, a_send.at[k, m], a_recv.at[me, m], dp=spread(k))

    @pl.loop(0, MICRO)
    def _(m):
        part = tile(m, block)

        @pl.when(section < sections - 1)
        def _():
            r_copy(m).wait_recv()

            @pl.loop(0, kv // 256)
            def _(n):
                dh[part, tile(n, 256)] = jnp.dot(
                    cot[part, :], w_full[:, tile(n, 256)], preferred_element_type=jnp.float32
                )

        help_later(2 * m)
        a = act[part, :]
        sig = jax.nn.sigmoid(a)
        grad_a = dh[part, :] * sig * (1.0 + a * (1.0 - sig))
        da_full[tile(me * MICRO + m, block), :] = (weight[part, :] * grad_a).astype(jnp.bfloat16)
        low = grad_a.astype(jnp.bfloat16)

        def back(j, sums):
            grad_n = lax.dot_general(
                low,
                w_full[tile(j, depth), :],
                (((1,), (1,)), ((), ())),
                preferred_element_type=jnp.float32,
            )
            u = gamma_ref[:, tile(j, depth)] * grad_n
            scaled[:, tile(j, depth)] = u
            xs = x_ref[part, tile(j, depth)].astype(jnp.float32)
            return sums + jnp.sum(xs * u, axis=1, keepdims=True)

        sums = lax.fori_loop(0, devices, back, jnp.zeros((block, 1), jnp.float32))
        r = inverse[part, :]
        cube = r * r * r * (sums / width)

        @pl.loop(0, devices)
        def _(j):
            cols = tile(j, depth)
            xs = x_ref[part, cols].astype(jnp.float32)
            g = cot[part, cols].astype(jnp.float32)
            passed[part, cols] = (g + r * scaled[:, cols] - xs * cube).astype(jnp.bfloat16)

        @pl.when(section > 0)
        def _():
            r_copy(m).start()

        @pl.loop(0, devices)
        def _(j):
            cols = tile(j, depth)
            w = weight[part, :]
            w_cot[part, cols] = (w * cot[part, cols].astype(jnp.float32)).astype(jnp.bfloat16)
            sg_ref[part, cols] = (w * passed[part, cols].astype(jnp.float32)).astype(jnp.bfloat16)

        g_col[tile(me * MICRO + m, block), :] = w_cot[part, tile(me, depth)]
        help_later(2 * m + 1)

        def hand_out(n):
            for k in range(near_by + 1):
                a_copy(k, n).start()
            for k in range(1, devices):
                g_copy(k, n).start()

        @pl.when(is_top & (m == 1))
        def _():
            share_hidden()
            share_normed()
            hand_out(0)

        @pl.when(jnp.logical_not(is_top) | (m > 0))
        def _():
            hand_out(m)

        @pl.when(m == jnp.where(is_top, MICRO - 1, 1))
        def _():
            h_onward()

        @pl.when((section == 0) & (m > 0))
        def _():
            a_onward(m - 1)

    @pl.when(section > 0)
    def _():
        @pl.loop(0, MICRO - 1)
        def _(m):
            a_onward(m)

    a_onward(MICRO - 1)

    def fh_copy(k, src):
        view = hid_full.at[tile(src, rows)]
        return remote(view, view, f_send.at[MICRO, k], f_recv.at[MICRO, k], dp=sibling)

    def fa_copy(k, src, m):
        view = da_full.at[tile(src * MICRO + m, block)]
        return remote(view, view, f_send.at[m, k], f_recv.at[m, k], dp=sibling)

    def far(k):
        return lax.rem(chip + k, chips) // near_by != side

    def h_settle(j, seen):
        @pl.when(jnp.logical_not(seen))
        def _():
            h_arrived(j)

    def a_settle(j, m, seen):
        @pl.when(jnp.logical_not(seen))
        def _():
            a_arrived(j, m)

    for k in range(1, chips):
        h_settle(peer(k), is_near & far(k))
        fh_copy(k, peer(k)).start()
    for k in range(1, devices):
        j = other(k)
        view = n_col.at[tile(j, rows)]
        remote(view, view, n_send.at[k], n_recv.at[j], dp=sibling).wait_recv()

    @pl.loop(0, devices)
    def _(j):
        n_colt[:, tile(j, rows)] = n_col[tile(j, rows), :].T

    @pl.loop(0, MICRO)
    def _(m):
        for k in range(1, chips):
            a_settle(peer(k), m, is_near & far(k))
            fa_copy(k, peer(k), m).start()

    h_arrived(sibling)
    for m in range(MICRO):
        a_arrived(sibling, m)

    for k in range(1, devices):
        j = other(k)
        for m in range(MICRO):
            view = g_col.at[tile(j * MICRO + m, block)]
            remote(view, view, g_send.at[k, m], g_recv.at[j, m], dp=sibling).wait_recv()

    @pl.loop(0, devices)
    def _(j):
        g_colt[:, tile(j, rows)] = g_col[tile(j, rows), :].T

    for k in range(1, chips):
        far = lax.rem(chip + k, chips) * 2 + (1 - core)
        fh_copy(k, far).wait_recv()

    @pl.loop(0, kv // 256)
    def _(n):
        cols = tile(n, 256)
        wg_ref[:, cols] = jnp.dot(g_colt[...], hid_full[:, cols], preferred_element_type=jnp.float32)

    @pl.loop(0, MICRO)
    def _(m):
        for k in range(1, chips):
            far = lax.rem(chip + k, chips) * 2 + (1 - core)
            fa_copy(k, far, m).wait_recv()

    @pl.loop(0, kv // 256)
    def _(n):
        cols = tile(n, 256)
        grad = jnp.dot(n_colt[...], da_full[:, cols], preferred_element_type=jnp.float32)
        wg_ref[:, cols] = (grad + wg_ref[:, cols]) / devices

    for k in range(1, devices):
        s_copy(k).wait_send()
        n_copy(k).wait_send()
        for m in range(MICRO):
            g_copy(k, m).wait_send()
    for k in range(near_by + 1):
        h_copy(k).wait_send()
        for m in range(MICRO):
            a_copy(k, m).wait_send()

    @pl.when(is_near)
    def _():
        for q in range(near_by):
            for k in range(1, near_by):
                hf_copy(q, k).wait_send()
                for m in range(MICRO):
                    af_copy(q, k, m).wait_send()

    for k in range(1, chips):
        fh_copy(k, peer(k)).wait_send()
        for m in range(MICRO):
            fa_copy(k, peer(k), m).wait_send()

    @pl.when(section > 0)
    def _():
        for m in range(MICRO):
            r_copy(m).wait_send()

    def line_left(across, their):
        v_out(across).wait_send()

        @pl.when(chip + 1 < chips)
        def _():
            w_own(0, across, up).wait_send()
            v_along(0, chip, their, up).wait_send()

        @pl.when(chip > 0)
        def _():
            w_own(1, across, down).wait_send()
            v_along(1, chip, their, down).wait_send()

        for hop in range(1, chips):
            below, above = me - 2 * hop, me + 2 * hop

            @pl.when(chip >= hop)
            def _():
                @pl.when(chip + 1 < chips)
                def _():
                    w_home(0, below, across, up).wait_send()
                    v_along(0, chip - hop, their, up).wait_send()

                w_side(below).wait_send()
                v_back(chip - hop, their).wait_send()

            @pl.when(chip + hop < chips)
            def _():
                @pl.when(chip > 0)
                def _():
                    w_home(1, above, across, down).wait_send()
                    v_along(1, chip + hop, their, down).wait_send()

                w_side(above).wait_send()
                v_back(chip + hop, their).wait_send()

    @pl.when(early)
    def _():
        line_left(across_early, across_late)

    @pl.when(jnp.logical_not(early))
    def _():
        line_left(across_late, across_early)

    w_side_own().wait_send()


def fused(
    section_inputs,
    gains,
    value_weight,
    top_cotangent,
    proxy_loss,
    reference_loss,
    lengths,
    doc_domain,
    log_weights,
    step_count,
):
    devices = lax.axis_size("dp")
    sections = lax.axis_size("section")
    rows, width = top_cotangent.shape
    depth, kv = value_weight.shape[1:]
    bf, f32 = jnp.bfloat16, jnp.float32
    chips = devices // 2
    dma = pltpu.SemaphoreType.DMA
    flops = 2 * rows * width * kv * 5
    vmem = pl.BlockSpec(memory_space=pltpu.VMEM)
    smem = pl.BlockSpec(memory_space=pltpu.SMEM)
    any_space = pl.BlockSpec(memory_space=pl.ANY)
    near_by = chips // 2
    section_grad, grad_shard, new_log = pl.pallas_call(
        functools.partial(relay_kernel, devices, sections),
        out_shape=(
            jax.ShapeDtypeStruct((rows, width), bf),
            jax.ShapeDtypeStruct((depth, kv), f32),
            jax.ShapeDtypeStruct((1, DOMAINS), f32),
        ),
        in_specs=[any_space, vmem, any_space, any_space, vmem, vmem, vmem, smem, smem, smem],
        out_specs=(vmem,) * 3,
        scratch_shapes=[
            pltpu.VMEM((rows, width), bf),
            pltpu.VMEM((width, kv), bf),
            pltpu.VMEM((rows, width), bf),
            pltpu.VMEM((rows, width), bf),
            pltpu.VMEM((rows, width), bf),
            pltpu.VMEM((rows, width), bf),
            pltpu.VMEM((rows, kv), f32),
            pltpu.VMEM((rows, kv), f32),
            pltpu.VMEM((rows // MICRO, width), f32),
            pltpu.VMEM((rows, 1), f32),
            pltpu.VMEM((rows, 1), f32),
            pltpu.VMEM((8, LANES), f32),
            pltpu.VMEM((devices, 8, LANES), f32),
            pltpu.VMEM((rows * devices, kv), bf),
            pltpu.VMEM((rows * devices, kv), bf),
            pltpu.VMEM((rows * devices, depth), bf),
            pltpu.VMEM((rows * devices, depth), bf),
            pltpu.VMEM((depth, rows * devices), bf),
            pltpu.VMEM((depth, rows * devices), bf),
            dma((3, devices)),
            dma((3, devices)),
            dma((devices,)),
            dma((devices,)),
            dma((devices,)),
            dma((devices,)),
            dma((near_by + 1,)),
            dma((devices,)),
            dma((devices, MICRO)),
            dma((devices, MICRO)),
            dma((near_by + 1, MICRO)),
            dma((devices, MICRO)),
            dma((MICRO + 1, chips)),
            dma((MICRO + 1, chips)),
            dma((MICRO,)),
            dma((MICRO,)),
            dma((near_by, near_by)),
            dma((near_by, near_by, MICRO)),
            dma((3,)),
            dma((4, chips)),
            dma((chips,)),
            pltpu.VMEM((chips, depth // 2, kv), bf),
        ],
        compiler_params=pltpu.CompilerParams(
            collective_id=0, has_side_effects=True, vmem_limit_bytes=60 * 2**20
        ),
        cost_estimate=pl.CostEstimate(
            flops=flops, bytes_accessed=2 * width * kv, transcendentals=rows * kv
        ),
    )(
        section_inputs[0],
        gains,
        value_weight[0],
        top_cotangent,
        proxy_loss[None],
        reference_loss[None],
        log_weights[None],
        lengths,
        doc_domain,
        step_count,
    )
    return (section_grad[None], grad_shard[None], new_log[0])


def choose(*args):
    depth, kv = args[2].shape[1:]
    devices = lax.axis_size("dp")
    held = 2 * kv * (depth * devices + 2 * args[3].shape[0] * devices)
    if devices % 4 == 0 and lax.axis_size("section") % 2 == 0 and depth % LANES == 0 and held <= 2**24:
        return fused(*args)
    return local(*args)


def solution(mesh):
    return jax.shard_map(
        choose,
        mesh=mesh,
        in_specs=(
            P("section", "dp", None),
            P("section", None),
            P("section", "dp", None),
            P("dp", None),
            P("dp"),
            P("dp"),
            P("dp", None),
            P("dp", None),
            P(),
            P(),
        ),
        out_specs=(P("section", "dp", None), P("section", "dp", None), P()),
        check_vma=False,
    )
```
